32 devices in a mesh: chan: 4 (over y, core), facet: 8 (over z, x).
Axes of the slice: x: 2, y: 2, z: 4, core: 2. Of those that a mesh axis runs over, the one named last changes fastest.
Arguments:
- visibilities: bfloat16 [16, 8, 4, 32768], P(None, None, 'chan', 'facet'), may hold values from -6 to 6
- w_kernel: bfloat16 [32, 2, 8], replicated, may hold values from -2 to 2
- w_index: int32 [4, 32768], P(None, 'facet'), may hold values from 0 to 31
- cell_offsets: int32 [2, 4, 32768], P(None, None, 'facet'), may hold values from 0 to 24
- block_sub: int32 [4, 64], P(None, 'facet'), may hold values from 0 to 31
- intersection_rows: int32 [8, 32], replicated, may hold values from 0 to 63, as said below
- intersection_count: int32 [8], replicated, may hold values from 1 to 32, as said below
Outputs:
- sky_image: float32 [16, 4, 64, 16384], P('chan', None, None, 'facet')
The draws below stay inside these ranges and needn't reach their ends.
Inputs may be any that keep to these rules, and one draw needn't show every extreme that they name: `intersection_rows`: the rows in one facet's list are distinct. `intersection_count`: some facet other than the last has exactly 32 entries in use.
All inputs are finite; a program needn't handle non-finite values.
Results may differ from the reference program's by a relative error of at most 0.0059.
Values may be sent and summed in bfloat16 or wider, within the bound.
No kernel may reach another device: no remote copies, remote signals or barrier semaphores. Data moves between devices by JAX's collectives and lax.ppermute only.
A program may use at most 128 MiB of HBM per device.

```python
import math
import jax
import jax.numpy as jnp
import numpy as np
from jax import lax

POL = 4
ROWS_DEV = 4096
BLK = 512
SG = 32
KS = 8
W = 32
NSUB = 32
FX = 2048
FY = 64
MARGIN = 128
MAXS = 32
GROUPS = 4
FACETS = 8
CHANS = 16
ROWS = 32768
BLOCKS = 64
NX = 16384


def draw_intersection_rows(key, part):
    facet_keys = jax.random.split(key, FACETS)

    def one_facet(sub_key):
        return jax.random.permutation(sub_key, FY)[:MAXS]
    return jax.vmap(one_facet)(facet_keys).astype(jnp.int32)


def draw_intersection_count(key, part):
    count_key, full_key = jax.random.split(jax.random.fold_in(key, 7))
    counts = jax.random.randint(count_key, (FACETS,), 1, MAXS + 1)
    full_facet = jax.random.randint(full_key, (), 0, FACETS - 1)
    return jnp.where(jnp.arange(FACETS) == full_facet, MAXS, counts).astype(jnp.int32)


def touch_ends(array, own_key, smallest, largest):
    shape = array.shape
    spot = [jax.random.randint(jax.random.fold_in(own_key, axis), (), 0, shape[axis]) for axis in range(len(shape))]
    array = array.at[tuple(spot)].set(smallest)
    longest = shape.index(max(shape))
    spot[longest] = (spot[longest] + 1) % shape[longest]
    return array.at[tuple(spot)].set(largest)


def level_of(stream_key, shape, cuts, low, top_value):
    factor_of = 1.0
    for dim, shards_of in cuts:
        draws = jax.random.uniform(jax.random.fold_in(jax.random.fold_in(stream_key, 6), dim), (shards_of,), jnp.float32, low / len(cuts), top_value / len(cuts))
        factor_of = factor_of * jnp.repeat(jnp.exp(draws), shape[dim] // shards_of).reshape((-1,) + (1,) * (len(shape) - 1 - dim))
    return factor_of


def rank_table(amount, slope):
    loads = [(1 << 20) // math.isqrt(grade ** slope) + 1 for grade in range(1, amount + 1)]
    scale = 1 + sum(loads) // (1 << 30)
    return np.cumsum(np.array([max(1, weight // scale) for weight in loads]))


def ranked_ids(rng, extent, number_of, slope):
    listing = rank_table(number_of, slope)
    pick = jax.random.randint(jax.random.fold_in(rng, 1), extent, 0, int(listing[number_of - 1]))
    standing = jnp.searchsorted(jnp.asarray(listing, jnp.int32), pick, side="right")
    return jax.random.permutation(jax.random.fold_in(rng, 2), number_of)[standing].astype(jnp.int32)


def noise(rng, shape, deviation, bound, cuts=(), kind=jnp.bfloat16):
    factor_of = level_of(rng, shape, cuts, -0.22, 0.18) if cuts else 1.0
    array = jax.random.normal(rng, shape, jnp.float32) * deviation * factor_of
    return jnp.minimum(jnp.maximum(array, -bound), bound).astype(kind)


def setup_inputs(seed: int = 0) -> dict:
    splits = jax.random.split(jax.random.key(seed), 8)
    return {
        "visibilities": noise(splits[0], (CHANS, 2 * POL, GROUPS, ROWS), 1.0, 6.0, ((2, 4), (3, 8))),
        "w_kernel": noise(splits[1], (W, 2, KS), KS ** -0.5, 2.0),
        "w_index": touch_ends(jax.random.randint(splits[2], (GROUPS, ROWS), 0, W), jax.random.fold_in(splits[2], 1), 0, W - 1).astype(jnp.int32),
        "cell_offsets": touch_ends(jax.random.randint(splits[3], (2, GROUPS, ROWS), 0, SG - KS + 1), jax.random.fold_in(splits[3], 1), 0, SG - KS).astype(jnp.int32),
        "block_sub": touch_ends(ranked_ids(splits[4], (GROUPS, BLOCKS), NSUB, 2), jax.random.fold_in(splits[4], 3), 0, NSUB - 1).astype(jnp.int32),
        "intersection_rows": draw_intersection_rows(jax.random.fold_in(splits[7], 71), 0),
        "intersection_count": draw_intersection_count(jax.random.fold_in(splits[7], 71), 0),
    }


def anchors(sub_index, side_len, period):
    span = period // side_len
    row_anchor = (jnp.mod(sub_index * 37, span) - span // 2) * side_len
    col_anchor = (jnp.mod(sub_index * 53 + 5, span) - span // 2) * side_len
    return (row_anchor, col_anchor)

def row_tables(sub_index, side_len, height, period):
    row_anchor, col_anchor = anchors(sub_index, side_len, period)
    cell_ids = jnp.arange(side_len, dtype=jnp.int32)
    line_ids = jnp.arange(height, dtype=jnp.int32) - height // 2
    phase_int = (row_anchor[:, None, None] + cell_ids[None, None, :]) * line_ids[None, :, None]
    radians = jnp.mod(phase_int, period).astype(jnp.float32) * (2.0 * math.pi / period)
    return (jnp.cos(radians).astype(jnp.bfloat16), jnp.sin(radians).astype(jnp.bfloat16))

def col_tables(sub_index, side_len, col_ids, period):
    row_anchor, col_anchor = anchors(sub_index, side_len, period)
    cell_ids = jnp.arange(side_len, dtype=jnp.int32)
    phase_int = (col_anchor[:, None, None] + cell_ids[None, :, None]) * (col_ids - period // 2)[None, None, :]
    radians = jnp.mod(phase_int, period).astype(jnp.float32) * (2.0 * math.pi / period)
    return (jnp.cos(radians).astype(jnp.bfloat16), (-jnp.sin(radians)).astype(jnp.bfloat16))

def place_kernel(values, offsets, side_len):
    distance = jnp.arange(side_len, dtype=jnp.int32)[:, None] - offsets[None, :]
    running = jnp.zeros((values.shape[0], side_len, offsets.shape[0]), jnp.float32)
    for tap_idx in range(values.shape[1]):
        running = running + values[:, tap_idx, None, :] * (distance == tap_idx).astype(jnp.float32)[None]
    return running

def combine(products, side_len, row_width):
    real_part = products[:, :side_len, :row_width] - products[:, side_len:, row_width:]
    imag_part = products[:, :side_len, row_width:] + products[:, side_len:, :row_width]
    return jnp.stack([real_part, imag_part], axis=1)

def block_terms(vis_part, plane_ids, cell_pos, kernel, side_len, block_len):
    planes = kernel.shape[0]
    plane_pick = (jnp.arange(planes, dtype=jnp.int32)[:, None] == plane_ids[None, :]).astype(jnp.float32)
    values = jnp.einsum('wqk,wr->qkr', kernel.astype(jnp.float32), plane_pick, precision=lax.Precision.HIGHEST)
    left_kern = place_kernel(values, cell_pos[0], side_len).astype(jnp.bfloat16)
    right_kern = place_kernel(values, cell_pos[1], side_len)
    num_pols = vis_part.shape[1] // 2
    vis_real = vis_part[:, :num_pols].astype(jnp.float32)[:, :, None, :]
    vis_imag = vis_part[:, num_pols:].astype(jnp.float32)[:, :, None, :]
    y_real = (vis_real * right_kern[0][None, None] - vis_imag * right_kern[1][None, None]).astype(jnp.bfloat16)
    y_imag = (vis_real * right_kern[1][None, None] + vis_imag * right_kern[0][None, None]).astype(jnp.bfloat16)
    num_rows = plane_ids.shape[0]
    blocks = num_rows // block_len
    row_width = vis_part.shape[0] * num_pols * side_len
    stacked = jnp.concatenate([y_real.reshape(row_width, blocks, block_len), y_imag.reshape(row_width, blocks, block_len)], axis=0)
    left_flat = left_kern.reshape(2 * side_len, blocks, block_len)
    products = lax.dot_general(left_flat.astype(jnp.float32), stacked.astype(jnp.float32), (((2,), (2,)), ((1,), (1,))), precision=lax.Precision.HIGHEST, preferred_element_type=jnp.float32)
    return combine(products, side_len, row_width)

def to_rows(subgrid, row_cos, row_sin, img_scale):
    sub_real = subgrid[:, 0].astype(jnp.float32)
    sub_imag = subgrid[:, 1].astype(jnp.float32)
    cos_full = row_cos.astype(jnp.float32)
    sin_full = row_sin.astype(jnp.float32)

    def apply_table(table, data):
        return jnp.einsum('gyu,guq->gyq', table, data, precision=lax.Precision.HIGHEST)
    real_part = apply_table(cos_full, sub_real) - apply_table(sin_full, sub_imag)
    imag_part = apply_table(cos_full, sub_imag) + apply_table(sin_full, sub_real)
    return (jnp.stack([real_part, imag_part], axis=1) * img_scale).astype(jnp.bfloat16)

def reference(visibilities, w_kernel, w_index, cell_offsets, block_sub, intersection_rows, intersection_count):
    per_dev = ROWS_DEV // BLK
    row_width = CHANS * POL * SG

    def grid_step(running, segment):
        group_id = segment // FACETS
        row_start = segment % FACETS * ROWS_DEV
        vis_part = lax.dynamic_index_in_dim(visibilities, group_id, 2, keepdims=False)
        vis_part = lax.dynamic_slice_in_dim(vis_part, row_start, ROWS_DEV, 2)
        plane_ids = lax.dynamic_slice_in_dim(lax.dynamic_index_in_dim(w_index, group_id, 0, keepdims=False), row_start, ROWS_DEV, 0)
        cell_pos = lax.dynamic_slice_in_dim(lax.dynamic_index_in_dim(cell_offsets, group_id, 1, keepdims=False), row_start, ROWS_DEV, 1)
        sub_ids = lax.dynamic_slice_in_dim(lax.dynamic_index_in_dim(block_sub, group_id, 0, keepdims=False), row_start // BLK, per_dev, 0)
        block_sums = block_terms(vis_part, plane_ids, cell_pos, w_kernel, SG, BLK)
        plane_pick = (jnp.arange(NSUB, dtype=jnp.int32)[:, None] == sub_ids[None, :]).astype(jnp.float32)
        increment = jnp.dot(plane_pick, block_sums.reshape(per_dev, 2 * SG * row_width), precision=lax.Precision.HIGHEST)
        return (running + increment, None)
    grid_init = jnp.zeros((NSUB, 2 * SG * row_width), jnp.float32)
    running, unused = lax.scan(grid_step, grid_init, jnp.arange(GROUPS * FACETS, dtype=jnp.int32))
    subgrid = running.reshape(NSUB, 2, SG, row_width).astype(jnp.bfloat16)
    sub_index = jnp.arange(NSUB, dtype=jnp.int32)
    row_cos, row_sin = row_tables(sub_index, SG, FY, NX)
    img_scale = 1.0 / math.sqrt(GROUPS * ROWS)
    row_image = to_rows(subgrid, row_cos, row_sin, img_scale)
    row_split = row_image.reshape(NSUB, 2, FY, CHANS * POL, SG).astype(jnp.float32)

    def facet_image(facet_id):
        col_ids = facet_id * FX + jnp.arange(FX, dtype=jnp.int32)
        col_cos, col_sin = col_tables(sub_index, SG, col_ids, NX)
        col_table = jnp.stack([col_cos, col_sin], axis=1).astype(jnp.float32)
        return jnp.einsum('grycv,grvx->cyx', row_split, col_table, precision=lax.Precision.HIGHEST)
    images = lax.map(facet_image, jnp.arange(FACETS, dtype=jnp.int32))
    line_ids = jnp.arange(FY, dtype=jnp.int32)
    slot_ids = jnp.arange(MAXS, dtype=jnp.int32)
    chosen = ((intersection_rows[:, :, None] == line_ids[None, None, :]) & (slot_ids[None, :, None] < intersection_count[:, None, None])).astype(jnp.float32)
    row_keep = lax.optimization_barrier(jnp.sum(chosen, axis=1))
    sent_band = images[:, :, :, FX - MARGIN:] * row_keep[:, None, :, None]
    arrived = jnp.concatenate([jnp.zeros_like(sent_band[:1]), sent_band[:-1]], axis=0)
    sky_image = jnp.concatenate([images[:, :, :, :MARGIN] + arrived, images[:, :, :, MARGIN:]], axis=3)
    sky_image = sky_image.reshape(FACETS, CHANS, POL, FY, FX).transpose(1, 2, 3, 0, 4)
    return sky_image.reshape(CHANS, POL, FY, NX)
```

```python
import functools
import math

import jax
import jax.numpy as jnp
from jax import lax
from jax.experimental import pallas as pl
from jax.experimental.pallas import tpu as pltpu
from jax.sharding import Mesh
from jax.sharding import PartitionSpec as P

BLK = 512
SG = 32
NSUB = 32
FX = 2048
FY = 64
MARGIN = 128
LANES = 128
PACK = LANES // SG
SETS = NSUB // PACK
CHAN = ("y", "core")
FACET = ("z1", "z0", "x")


def swap(block, axis):
    return shift(block, axis, 1)


def shift(block, axis, distance):
    size = lax.axis_size(axis)
    return lax.ppermute(block, axis, [(i, (i + distance) % size) for i in range(size)])


def grid_kernel(place_ref, sub_ref, taps_ref, rows_ref, *refs, row_len):
    out_refs, sums_ref = refs[:-1], refs[-1]
    step = pl.program_id(0)
    lines = rows_ref.shape[1]
    pols = lines // 4
    half = pols // 2
    cells = 2 * pols * SG
    blocks = row_len // BLK
    pieces = lines // blocks
    width = row_len // lines

    @pl.when(step == 0)
    def _():
        sums_ref[...] = jnp.zeros_like(sums_ref)

    taps = taps_ref[...]
    ids = rows_ref[0, :, row_len : row_len + 3 * width].astype(jnp.float32).astype(jnp.int32)
    cell = lax.broadcasted_iota(jnp.int32, (8, BLK), 0)
    line_id = lax.broadcasted_iota(jnp.int32, (lines, BLK), 0)

    def listed(kind, block):
        part = ids[:, kind * width : (kind + 1) * width]
        found = [part[k : k + 1] for k in range(pieces * block, pieces * (block + 1))]
        return jnp.concatenate(found, axis=1) if pieces > 1 else found[0]

    def pick(values, index, axis):
        found = [
            jnp.take_along_axis(
                values if axis else values[:, c : c + LANES], index[:, c : c + LANES], axis=axis
            )
            for c in range(0, BLK, LANES)
        ]
        return jnp.concatenate(found, axis=1)

    def spread(values, offset):
        distance = cell - offset
        keep = [
            (distance + 8 * tile >= 0) & (distance + 8 * tile < 8) for tile in range(SG // 8)
        ]
        turned = [pick(values[8 * q : 8 * q + 8], distance & 7, 0) for q in range(2)]
        return [
            jnp.concatenate([jnp.where(m, part, 0.0) for m in keep], axis=0) for part in turned
        ]

    for block in range(blocks):
        plane = jnp.broadcast_to(listed(0, block), (16, BLK))
        values = pick(taps, plane, 1)
        left = jnp.concatenate(spread(values, listed(1, block)), axis=0).astype(jnp.bfloat16)
        kern_re, kern_im = spread(values, listed(2, block))
        vis = rows_ref[0, :, block * BLK : (block + 1) * BLK].astype(jnp.float32)
        vis = pltpu.roll(vis, place_ref[0] * (lines // 2), 0)
        turned = jnp.where(
            line_id % pols < half, pltpu.roll(vis, lines - half, 0), pltpu.roll(vis, half, 0)
        )
        vis = jnp.where(place_ref[1] == 1, turned, vis)
        real, imag = [], []
        for first in (0, 2 * pols):
            for row in range(first, first + pols):
                vis_re = vis[row : row + 1]
                vis_im = vis[row + pols : row + pols + 1]
                real.append((vis_re * kern_re - vis_im * kern_im).astype(jnp.bfloat16))
                imag.append((vis_re * kern_im + vis_im * kern_re).astype(jnp.bfloat16))
        weighted = jnp.concatenate(real + imag, axis=0)
        sub = sub_ref[step * blocks + block]
        sums_ref[sub] += lax.dot_general(
            left, weighted, (((1,), (1,)), ((), ())), preferred_element_type=jnp.float32
        )

    @pl.when(step == pl.num_programs(0) - 1)
    def _():
        slot = lax.broadcasted_iota(jnp.int32, (2 * SG, LANES), 1) // SG

        def finish(group, carry):
            parts = []
            for k in range(PACK):
                raw = sums_ref[group * PACK + k]
                real = raw[:SG, :cells] - raw[SG:, cells:]
                imag = raw[:SG, cells:] + raw[SG:, :cells]
                parts.append(jnp.concatenate([real, imag], axis=0))
            for pol in range(2 * pols):
                tile = slice(pol // PACK * LANES, (pol // PACK + 1) * LANES)
                packed = jnp.zeros((2 * SG, LANES), jnp.float32)
                for k in range(PACK):
                    move = (k - pol) % PACK * SG
                    part = parts[k][:, tile]
                    part = pltpu.roll(part, move, 1) if move else part
                    packed = jnp.where(slot == k, part, packed)
                out_refs[pol // half][pol % half, group] = packed.astype(jnp.bfloat16)
            return carry

        lax.fori_loop(0, SETS, finish, 0)


def grid_rows(place, sub_ids, taps, rows, row_len):
    sources, lines, width = rows.shape
    pols = lines // 4
    shape = (pols // 2, SETS, 2 * SG, LANES)
    whole = pl.BlockSpec(shape, lambda s, *_: (0, 0, 0, 0))
    flops = 2 * sources * row_len * 2 * SG * 4 * pols * SG
    return pl.pallas_call(
        functools.partial(grid_kernel, row_len=row_len),
        out_shape=[jax.ShapeDtypeStruct(shape, jnp.bfloat16)] * 4,
        grid_spec=pltpu.PrefetchScalarGridSpec(
            num_scalar_prefetch=2,
            grid=(sources,),
            in_specs=[
                pl.BlockSpec(taps.shape, lambda s, *_: (0, 0)),
                pl.BlockSpec((1, lines, width), lambda s, *_: (s, 0, 0)),
            ],
            out_specs=[whole] * 4,
            scratch_shapes=[pltpu.VMEM((NSUB, 2 * SG, 4 * pols * SG), jnp.float32)],
        ),
        compiler_params=pltpu.CompilerParams(vmem_limit_bytes=32 << 20),
        cost_estimate=pl.CostEstimate(flops=flops, bytes_accessed=3 << 20, transcendentals=0),
        name="grid_rows",
    )(place, sub_ids, taps, rows)


def table_kernel(first_ref, out_ref, *, period):
    group = pl.program_id(0)
    cells = PACK * SG
    row = lax.broadcasted_iota(jnp.int32, (cells, LANES), 0)
    lane = lax.broadcasted_iota(jnp.int32, (cells, LANES), 1)
    span = period // SG
    sub = group * PACK + row // SG
    cell = (lax.rem(sub * 53 + 5, span) - span // 2) * SG + row % SG
    unit = 2.0 * math.pi / period

    def angle(column):
        return jnp.mod(cell * column, period).astype(jnp.float32) * unit

    tiles = out_ref.shape[1] // LANES
    start = jnp.where(lane == tiles - 1, -MARGIN, lane * LANES)
    fine, coarse = angle(lane), angle(first_ref[0] + start)
    fine_cos, fine_sin = jnp.cos(fine), jnp.sin(fine)
    coarse_cos, coarse_sin = jnp.cos(coarse), jnp.sin(coarse)
    for tile in range(tiles):
        columns = slice(tile * LANES, (tile + 1) * LANES)
        tile_cos = coarse_cos[:, tile : tile + 1]
        tile_sin = coarse_sin[:, tile : tile + 1]
        full_cos = tile_cos * fine_cos - tile_sin * fine_sin
        full_sin = tile_sin * fine_cos + tile_cos * fine_sin
        out_ref[:cells, columns] = full_cos.astype(jnp.bfloat16)
        out_ref[cells:, columns] = (-full_sin).astype(jnp.bfloat16)


def col_table(first, period, width):
    depth = 2 * NSUB * SG
    return pl.pallas_call(
        functools.partial(table_kernel, period=period),
        out_shape=jax.ShapeDtypeStruct((depth, width), jnp.bfloat16),
        grid_spec=pltpu.PrefetchScalarGridSpec(
            num_scalar_prefetch=1,
            grid=(SETS,),
            in_specs=[],
            out_specs=pl.BlockSpec((depth // SETS, width), lambda g, *_: (g, 0)),
        ),
        cost_estimate=pl.CostEstimate(
            flops=8 * depth * width, bytes_accessed=2 * depth * width, transcendentals=1 << 19
        ),
        name="col_table",
    )(first)


def row_table(period):
    sub = jnp.arange(NSUB, dtype=jnp.int32)
    span = period // SG
    anchor = (jnp.mod(sub * 37, span) - span // 2) * SG
    cell_ids = jnp.arange(SG, dtype=jnp.int32)
    line_ids = jnp.arange(FY, dtype=jnp.int32) - FY // 2
    phase = (anchor[:, None, None] + cell_ids[None, None, :]) * line_ids[None, :, None]
    radians = jnp.mod(phase, period).astype(jnp.float32) * (2.0 * math.pi / period)
    cos, sin = jnp.cos(radians), jnp.sin(radians)
    turn = jnp.stack([jnp.stack([cos, -sin], 2), jnp.stack([sin, cos], 2)], 1)
    turn = turn.reshape(SETS, PACK, 2 * FY, 2 * SG).transpose(0, 2, 1, 3)
    return turn.reshape(SETS, 2 * FY, PACK * 2 * SG).astype(jnp.bfloat16)


def image_kernel(place_ref, *refs, parts, scale):
    piece_refs = refs[:parts]
    turn_ref, table_ref, edge_ref, keep_ref = refs[parts : parts + 4]
    out_ref, rows_ref = refs[-2:]
    step = pl.program_id(0)
    per = piece_refs[0].shape[0]
    columns = out_ref.shape[2]

    @pl.when(step == 0)
    def _():
        slot = lax.broadcasted_iota(jnp.int32, (2 * SG, 2 * LANES), 1) % LANES // SG
        flat = [(part, i) for part in range(parts) for i in range(per)]

        def group_rows(group, carry):
            for k in range(0, len(flat), 2):
                pair = [piece_refs[part][i, group] for part, i in flat[k : k + 2]]
                pair = jnp.concatenate(pair, axis=1)
                zero = jnp.zeros_like(pair)
                spread = [jnp.where(slot == s, pair, zero) for s in range(PACK)]
                spread = jnp.concatenate(spread, axis=0)
                turned = jnp.dot(turn_ref[group], spread, preferred_element_type=jnp.float32)
                turned = (turned * scale).astype(jnp.bfloat16)
                for m in range(2):
                    for q in range(2):
                        rows_ref[
                            group, (k + m) * FY : (k + m + 1) * FY, q * LANES : (q + 1) * LANES
                        ] = turned[q * FY : (q + 1) * FY, m * LANES : (m + 1) * LANES]
            return carry

        lax.fori_loop(0, SETS, group_rows, 0)

    lines = jnp.concatenate([rows_ref[group] for group in range(SETS)], axis=1)
    total = jnp.dot(lines, table_ref[...], preferred_element_type=jnp.float32)
    total = total.reshape(parts * per, FY, columns)
    for part in range(parts):
        where = pl.ds(lax.rem(place_ref[1] + part, 2) * per, per)
        out_ref[where] = total[part * per : (part + 1) * per]

    @pl.when(step == 0)
    def _():
        edge = jnp.dot(lines, edge_ref[...], preferred_element_type=jnp.float32)
        edge = edge.reshape(parts * per, FY, MARGIN) * keep_ref[...][None]
        for part in range(parts):
            where = pl.ds(lax.rem(place_ref[1] + part, 2) * per, per)
            out_ref[where, :, :MARGIN] += edge[part * per : (part + 1) * per]


def add_image(image, place, pieces, turn, table, keep, total_pols, scale):
    parts, per = len(pieces), pieces[0].shape[0]
    pols = parts * per
    columns = 512
    depth = table.shape[0]
    width = table.shape[1] - MARGIN

    def whole(array):
        return pl.BlockSpec(array.shape, lambda s, *_: (0,) * array.ndim)

    operands = [*pieces, turn, table, table, keep]
    in_specs = [whole(piece) for piece in pieces] + [
        whole(turn),
        pl.BlockSpec((depth, columns), lambda s, *_: (0, s)),
        pl.BlockSpec((depth, MARGIN), lambda s, *_: (0, width // MARGIN)),
        whole(keep),
    ]
    aliases = {}
    if image is not None:
        operands.append(image)
        in_specs.append(pl.BlockSpec(memory_space=pl.ANY))
        aliases = {len(operands): 0}
    return pl.pallas_call(
        functools.partial(image_kernel, parts=parts, scale=scale),
        out_shape=jax.ShapeDtypeStruct((total_pols, FY, width), jnp.float32),
        grid_spec=pltpu.PrefetchScalarGridSpec(
            num_scalar_prefetch=1,
            grid=(width // columns,),
            in_specs=in_specs,
            out_specs=pl.BlockSpec((pols, FY, columns), lambda s, place: (place[0], 0, s)),
            scratch_shapes=[pltpu.VMEM((SETS, pols * FY, 2 * LANES), jnp.bfloat16)],
        ),
        input_output_aliases=aliases,
        compiler_params=pltpu.CompilerParams(vmem_limit_bytes=32 << 20),
        cost_estimate=pl.CostEstimate(
            flops=2 * pols * FY * depth * width,
            bytes_accessed=2 * depth * width + 4 * pols * FY * width,
            transcendentals=0,
        ),
        name="add_image",
    )(place, *operands)


def shards(
    visibilities, w_kernel, w_index, cell_offsets, block_sub, intersection_rows, intersection_count
):
    cores, east = lax.axis_size("core"), lax.axis_size("x")
    north, upper = lax.axis_size("y"), lax.axis_size("z0")
    groups, facets = north * cores, lax.axis_size(FACET)
    num_chans, num_parts, _, row_len = visibilities.shape
    num_pols = num_parts // 2
    own_chans = num_chans // groups
    shares = upper * east
    chan_shares = math.gcd(shares, own_chans)
    pol_shares = shares // chan_shares
    per_chan, per_pol = own_chans // chan_shares, num_pols // pol_shares
    pols = per_chan * per_pol
    lines = 4 * pols
    period = FX * facets
    facet_id = lax.axis_index(FACET)
    group_id = lax.axis_index(CHAN)
    core, z1, z0, x = (lax.axis_index(axis) for axis in ("core", "z1", "z0", "x"))

    vis = visibilities.reshape(
        north, cores, chan_shares, per_chan, 2, pol_shares, per_pol, row_len
    )
    vis = vis.transpose(0, 2, 5, 1, 4, 3, 6, 7).reshape(north * shares, lines, row_len)
    plane = lax.dynamic_slice_in_dim(w_index, group_id, 1, 0)
    cells = lax.dynamic_slice_in_dim(cell_offsets, group_id, 1, 1).reshape(2, row_len)
    ids = jnp.concatenate([plane, cells], axis=0).reshape(3, lines, row_len // lines)
    ids = ids.transpose(1, 0, 2).reshape(lines, 3 * row_len // lines)
    blocks = row_len // BLK
    subs = lax.dynamic_slice_in_dim(block_sub, group_id, 1, 0).reshape(blocks, 1, 1)
    subs = jnp.broadcast_to(subs, (blocks, lines // blocks, LANES)).reshape(lines, LANES)
    ids = jnp.concatenate([ids, subs], axis=1).astype(jnp.bfloat16)
    ids = jnp.broadcast_to(ids[None], (north * shares,) + ids.shape)
    sent = jnp.concatenate([vis, ids], axis=2)
    rows = lax.all_to_all(sent, ("y", "z0", "x"), split_axis=0, concat_axis=0, tiled=True)
    sub_ids = rows[:, :: lines // blocks, -1].astype(jnp.int32).reshape(-1)

    taps = w_kernel.astype(jnp.float32).transpose(1, 2, 0).reshape(-1, w_kernel.shape[0])
    taps = jnp.pad(taps, ((0, 0), (0, LANES - taps.shape[1])))
    first = jnp.reshape(facet_id * FX - period // 2, (1,)).astype(jnp.int32)
    table = col_table(first, period, FX + MARGIN)
    turn = row_table(period)

    ahead = jnp.maximum(facet_id - 1, 0)
    listed = lax.dynamic_index_in_dim(intersection_rows, ahead, 0, keepdims=False)
    in_use = lax.dynamic_index_in_dim(intersection_count, ahead, 0, keepdims=False)
    in_use = jnp.where(facet_id > 0, in_use, 0)
    line_ids = jnp.arange(FY, dtype=jnp.int32)
    slot_ids = jnp.arange(intersection_rows.shape[1], dtype=jnp.int32)
    keep = (listed[None, :] == line_ids[:, None]) & (slot_ids[None, :] < in_use)
    keep = jnp.sum(keep.astype(jnp.float32), axis=1, keepdims=True)
    keep = jnp.broadcast_to(keep, (FY, MARGIN))

    def total(*arrays):
        return sum(a.astype(jnp.float32) for a in arrays).astype(jnp.bfloat16)

    place = jnp.stack([core, z1]).astype(jnp.int32)
    keep_own, send_own, keep_other, send_other = grid_rows(place, sub_ids, taps, rows, row_len)
    far = total(send_own, swap(send_other, "core"))
    own = total(keep_own, swap(keep_other, "core"), swap(far, "z1"))
    scale = 1.0 / math.sqrt(groups * facets * row_len)

    image = None
    mine = [own, swap(own, "z1")]
    for z_step in range(upper):
        here = mine if z_step == 0 else [shift(piece, "z0", z_step) for piece in mine]
        for x_step in range(east):
            pieces = here if x_step == 0 else [shift(piece, "x", x_step) for piece in here]
            share = lax.rem(z0 + upper - z_step, upper) * east + lax.rem(x + east - x_step, east)
            spot = jnp.stack([share, z1]).astype(jnp.int32)
            image = add_image(
                image, spot, pieces, turn, table, keep, own_chans * num_pols, scale
            )
    return image.reshape(own_chans, num_pols, FY, FX)


def solution(mesh):
    groups, facets = mesh.shape["chan"], mesh.shape["facet"]
    inner = Mesh(
        mesh.devices.reshape(groups // 2, 2, 2, 2, facets // 4), CHAN + FACET
    )
    return jax.shard_map(
        shards,
        mesh=inner,
        in_specs=(
            P(None, None, CHAN, FACET),
            P(),
            P(None, FACET),
            P(None, None, FACET),
            P(None, FACET),
            P(),
            P(),
        ),
        out_specs=P(CHAN, None, None, FACET),
        check_vma=False,
    )
```

```python
import functools
import math

import jax
import jax.numpy as jnp
from jax import lax
from jax.experimental import pallas as pl
from jax.experimental.pallas import tpu as pltpu
from jax.sharding import Mesh
from jax.sharding import PartitionSpec as P

BLK = 512
SG = 32
NSUB = 32
FX = 2048
FY = 64
MARGIN = 128
LANES = 128
PACK = LANES // SG
SETS = NSUB // PACK
CHAN = ("y", "core")
FACET = ("z1", "z0", "x")


def swap(block, axis):
    return lax.ppermute(block, axis, [(0, 1), (1, 0)])


def pack_kernel(group_ref, vis_ref, plane_ref, cell_ref, sub_ref, first_ref, second_ref, *, shares):
    chan_shares, pol_shares, per_chan, per_pol, cores = shares
    num_pols = vis_ref.shape[1] // 2
    row_len = vis_ref.shape[2]
    lines = first_ref.shape[1]
    width = row_len // lines
    half = per_pol // 2
    group = group_ref[0]

    def folded(row):
        row = row.astype(jnp.float32)
        return jnp.concatenate([row[:, k * width : (k + 1) * width] for k in range(lines)], axis=0)

    subs = sub_ref[pl.ds(group, 1), :].astype(jnp.float32)
    subs = jnp.concatenate([subs, jnp.zeros((1, LANES - subs.shape[1]), jnp.float32)], axis=1)
    ids = [
        folded(plane_ref[pl.ds(group, 1), :]),
        folded(cell_ref[0, pl.ds(group, 1), :]),
        folded(cell_ref[1, pl.ds(group, 1), :]),
        jnp.broadcast_to(subs, (lines, LANES)),
    ]
    ids = jnp.concatenate(ids, axis=1).astype(jnp.bfloat16)
    dest = 0
    for north in range(first_ref.shape[0] // (chan_shares * pol_shares)):
        for chan_share in range(chan_shares):
            for pol_share in range(pol_shares):
                found = ([], [])
                for core in range(cores):
                    chans = (north * cores + core) * chan_shares + chan_share
                    chans = [
                        vis_ref[chans * per_chan + k].astype(jnp.float32) for k in range(per_chan)
                    ]
                    for part in range(2):
                        start = part * num_pols + pol_share * per_pol
                        for vis in chans:
                            found[0].append(vis[start : start + half])
                            found[1].append(vis[start + half : start + per_pol])
                first_ref[dest, :, :row_len] = jnp.concatenate(found[0], 0).astype(jnp.bfloat16)
                first_ref[dest, :, row_len:] = ids
                second_ref[dest] = jnp.concatenate(found[1], 0).astype(jnp.bfloat16)
                dest += 1


def pack_rows(group, vis, planes, cells, subs, shares, dests, lines):
    row_len = vis.shape[2]
    extra = 3 * row_len // lines + LANES
    vmem = pl.BlockSpec(memory_space=pltpu.VMEM)
    return pl.pallas_call(
        functools.partial(pack_kernel, shares=shares),
        out_shape=[
            jax.ShapeDtypeStruct((dests, lines, row_len + extra), jnp.bfloat16),
            jax.ShapeDtypeStruct((dests, lines, row_len), jnp.bfloat16),
        ],
        grid_spec=pltpu.PrefetchScalarGridSpec(
            num_scalar_prefetch=1, grid=(), in_specs=[vmem] * 4, out_specs=[vmem] * 2
        ),
        compiler_params=pltpu.CompilerParams(vmem_limit_bytes=24 << 20),
        cost_estimate=pl.CostEstimate(flops=1 << 20, bytes_accessed=3 << 20, transcendentals=0),
        name="pack_rows",
    )(group, vis, planes, cells, subs)


def grid_kernel(place_ref, sub_ref, taps_ref, ids_ref, rows_ref, *refs, row_len, ids_from):
    own_ref, other_ref, sums_ref = refs[-3:]
    step = pl.program_id(0)
    lines = rows_ref.shape[1]
    pols = lines // 4
    cells = 2 * pols * SG
    blocks = row_len // BLK
    width = row_len // lines

    @pl.when(step == 0)
    def _():
        sums_ref[...] = jnp.zeros_like(sums_ref)

    taps = taps_ref[...]
    ids = ids_ref[0, :, ids_from : ids_from + 3 * width].astype(jnp.float32).astype(jnp.int32)
    cell = lax.broadcasted_iota(jnp.int32, (8, BLK), 0)

    def listed(kind, block):
        found = []
        for start in range(block * BLK, (block + 1) * BLK, min(BLK, width)):
            line, column = start // width, kind * width + start % width
            found.append(ids[line : line + 1, column : column + min(BLK, width)])
        return jnp.concatenate(found, axis=1) if len(found) > 1 else found[0]

    def pick(values, index, axis):
        found = [
            jnp.take_along_axis(
                values if axis else values[:, c : c + LANES], index[:, c : c + LANES], axis=axis
            )
            for c in range(0, BLK, LANES)
        ]
        return jnp.concatenate(found, axis=1)

    def spread(values, offset):
        distance = cell - offset
        keep = [
            (distance + 8 * tile >= 0) & (distance + 8 * tile < 8) for tile in range(SG // 8)
        ]
        turned = [pick(values[8 * q : 8 * q + 8], distance & 7, 0) for q in range(2)]
        return [
            jnp.concatenate([jnp.where(m, part, 0.0) for m in keep], axis=0) for part in turned
        ]

    for block in range(blocks):
        plane = jnp.broadcast_to(listed(0, block), (16, BLK))
        values = pick(taps, plane, 1)
        left = jnp.concatenate(spread(values, listed(1, block)), axis=0).astype(jnp.bfloat16)
        kern_re, kern_im = spread(values, listed(2, block))
        vis = rows_ref[0, :, block * BLK : (block + 1) * BLK].astype(jnp.float32)
        vis = pltpu.roll(vis, place_ref[0] * (lines // 2), 0)
        real, imag = [], []
        for first in (0, 2 * pols):
            for row in range(first, first + pols):
                vis_re = vis[row : row + 1]
                vis_im = vis[row + pols : row + pols + 1]
                real.append((vis_re * kern_re - vis_im * kern_im).astype(jnp.bfloat16))
                imag.append((vis_re * kern_im + vis_im * kern_re).astype(jnp.bfloat16))
        weighted = jnp.concatenate(real + imag, axis=0)
        sub = sub_ref[step * blocks + block]
        sums_ref[sub] += lax.dot_general(
            left, weighted, (((1,), (1,)), ((), ())), preferred_element_type=jnp.float32
        )

    @pl.when(step == pl.num_programs(0) - 1)
    def _():
        slot = lax.broadcasted_iota(jnp.int32, (2 * SG, LANES), 1) // SG

        def finish(group, carry):
            parts = []
            for k in range(PACK):
                raw = sums_ref[group * PACK + k]
                real = raw[:SG, :cells] - raw[SG:, cells:]
                imag = raw[:SG, cells:] + raw[SG:, :cells]
                part = jnp.concatenate([real, imag], axis=0)
                if cells < LANES:
                    part = jnp.concatenate([part, jnp.zeros_like(part)], axis=1)
                parts.append(part)
            for pol in range(2 * pols):
                tile = slice(pol // PACK * LANES, (pol // PACK + 1) * LANES)
                packed = jnp.zeros((2 * SG, LANES), jnp.float32)
                for k in range(PACK):
                    move = (k - pol) % PACK * SG
                    part = parts[k][:, tile]
                    part = pltpu.roll(part, move, 1) if move else part
                    packed = jnp.where(slot == k, part, packed)
                out_ref = own_ref if pol < pols else other_ref
                out_ref[pol % pols, group] = packed.astype(jnp.bfloat16)
            return carry

        lax.fori_loop(0, SETS, finish, 0)


def grid_rows(place, sub_ids, taps, ids, rows, row_len, token):
    sources, lines, _ = rows.shape
    pols = lines // 4
    shape = (pols, SETS, 2 * SG, LANES)
    whole = pl.BlockSpec(shape, lambda s, *_: (0, 0, 0, 0))
    flops = 2 * sources * row_len * 2 * SG * 4 * pols * SG
    return pl.pallas_call(
        functools.partial(grid_kernel, row_len=row_len, ids_from=row_len),
        out_shape=[jax.ShapeDtypeStruct(shape, jnp.bfloat16)] * 2,
        grid_spec=pltpu.PrefetchScalarGridSpec(
            num_scalar_prefetch=2,
            grid=(sources,),
            in_specs=[
                pl.BlockSpec(taps.shape, lambda s, *_: (0, 0)),
                pl.BlockSpec((1,) + ids.shape[1:], lambda s, *_: (s, 0, 0)),
                pl.BlockSpec((1,) + rows.shape[1:], lambda s, *_: (s, 0, 0)),
                pl.BlockSpec(memory_space=pl.ANY),
            ],
            out_specs=[whole] * 2,
            scratch_shapes=[pltpu.VMEM((NSUB, 2 * SG, 4 * pols * SG), jnp.float32)],
        ),
        compiler_params=pltpu.CompilerParams(vmem_limit_bytes=16 << 20),
        cost_estimate=pl.CostEstimate(
            flops=flops * 8, bytes_accessed=2 << 20, transcendentals=0
        ),
        name="grid_rows",
    )(place, sub_ids, taps, ids, rows, token)


def tables_kernel(facet_ref, listed_ref, count_ref, table_ref, turn_ref, keep_ref, *, period):
    facet = facet_ref[0]
    span = period // SG
    unit = 2.0 * math.pi / period

    def angle(phase):
        return jnp.mod(phase, period).astype(jnp.float32) * unit

    cells = PACK * SG
    row = lax.broadcasted_iota(jnp.int32, (cells, LANES), 0)
    lane = lax.broadcasted_iota(jnp.int32, (cells, LANES), 1)
    tiles = table_ref.shape[1] // LANES
    start = facet * FX - period // 2 + jnp.where(lane == tiles - 1, -MARGIN, lane * LANES)
    turn_shape = (2 * FY, 2 * PACK * SG)
    turn_row = lax.broadcasted_iota(jnp.int32, turn_shape, 0)
    turn_lane = lax.broadcasted_iota(jnp.int32, turn_shape, 1)

    def group_tables(group, carry):
        sub = group * PACK + row // SG
        cell = (lax.rem(sub * 53 + 5, span) - span // 2) * SG + row % SG
        fine, coarse = angle(cell * lane), angle(cell * start)
        fine_cos, fine_sin = jnp.cos(fine), jnp.sin(fine)
        coarse_cos, coarse_sin = jnp.cos(coarse), jnp.sin(coarse)
        base = pl.multiple_of(group * 2 * cells, 2 * cells)
        for tile in range(tiles):
            columns = slice(tile * LANES, (tile + 1) * LANES)
            tile_cos = coarse_cos[:, tile : tile + 1]
            tile_sin = coarse_sin[:, tile : tile + 1]
            full_cos = tile_cos * fine_cos - tile_sin * fine_sin
            full_sin = tile_sin * fine_cos + tile_cos * fine_sin
            table_ref[pl.ds(base, cells), columns] = full_cos.astype(jnp.bfloat16)
            table_ref[pl.ds(base + cells, cells), columns] = (-full_sin).astype(jnp.bfloat16)
        sub = group * PACK + turn_lane // (2 * SG)
        cell = (lax.rem(sub * 37, span) - span // 2) * SG + turn_lane % SG
        quarter = turn_lane // SG % 2 - turn_row // FY
        phase = cell * (turn_row % FY - FY // 2) + quarter * (period // 4)
        turn_ref[group] = jnp.cos(angle(phase)).astype(jnp.bfloat16)
        return carry

    lax.fori_loop(0, SETS, group_tables, 0)
    line = lax.broadcasted_iota(jnp.int32, (FY, MARGIN), 0)
    before = jnp.maximum(facet - 1, 0)
    in_use = jnp.where(facet > 0, count_ref[before], 0)

    def mark(k, keep):
        return jnp.where((line == listed_ref[before, k]) & (k < in_use), 1.0, keep)

    keep_ref[...] = lax.fori_loop(
        0, listed_ref.shape[1], mark, jnp.zeros((FY, MARGIN), jnp.float32)
    )


def make_tables(facet, listed, counts, period):
    depth, width = 2 * NSUB * SG, FX + MARGIN
    vmem = pl.BlockSpec(memory_space=pltpu.VMEM)
    return pl.pallas_call(
        functools.partial(tables_kernel, period=period),
        out_shape=[
            jax.ShapeDtypeStruct((depth, width), jnp.bfloat16),
            jax.ShapeDtypeStruct((SETS, 2 * FY, 2 * PACK * SG), jnp.bfloat16),
            jax.ShapeDtypeStruct((FY, MARGIN), jnp.float32),
        ],
        grid_spec=pltpu.PrefetchScalarGridSpec(
            num_scalar_prefetch=3, grid=(), in_specs=[], out_specs=[vmem] * 3
        ),
        compiler_params=pltpu.CompilerParams(vmem_limit_bytes=16 << 20),
        cost_estimate=pl.CostEstimate(
            flops=8 * depth * width, bytes_accessed=2 * depth * width, transcendentals=1 << 19
        ),
        name="make_tables",
    )(facet, listed, counts)


def image_kernel(place_ref, *refs, parts, scale, columns):
    piece_refs = refs[:parts]
    turn_ref, table_ref, keep_ref = refs[parts : parts + 3]
    out_ref, lines_ref, done_ref, sems = refs[-4:]
    per = piece_refs[0].shape[0]
    width = table_ref.shape[1] - MARGIN
    slot = lax.broadcasted_iota(jnp.int32, (2 * SG, 2 * LANES), 1) % LANES // SG
    flat = [(part, i) for part in range(parts) for i in range(per)]

    def group_rows(group, carry):
        base = pl.multiple_of(group * 2 * LANES, 2 * LANES)
        for k in range(0, len(flat), 2):
            pair = [piece_refs[part][i, group] for part, i in flat[k : k + 2]]
            pair = jnp.concatenate(pair, axis=1)
            zero = jnp.zeros_like(pair)
            spread = [jnp.where(slot == s, pair, zero) for s in range(PACK)]
            spread = jnp.concatenate(spread, axis=0)
            turned = jnp.dot(turn_ref[group], spread, preferred_element_type=jnp.float32)
            turned = (turned * scale).astype(jnp.bfloat16)
            for m in range(2):
                for q in range(2):
                    lines_ref[
                        (k + m) * FY : (k + m + 1) * FY, pl.ds(base + q * LANES, LANES)
                    ] = turned[q * FY : (q + 1) * FY, m * LANES : (m + 1) * LANES]
        return carry

    lax.fori_loop(0, SETS, group_rows, 0)
    lines = lines_ref[...]

    def copy(step, part):
        return pltpu.make_async_copy(
            done_ref.at[step % 2, pl.ds(part * per, per)],
            out_ref.at[pl.ds(place_ref[part], per), :, pl.ds(step * columns, columns)],
            sems.at[step % 2, part],
        )

    steps = width // columns
    for step in range(steps):
        if step >= 2:
            for part in range(parts):
                copy(step - 2, part).wait()
        block = table_ref[:, step * columns : (step + 1) * columns]
        total = jnp.dot(lines, block, preferred_element_type=jnp.float32)
        done_ref[step % 2] = total.reshape(parts * per, FY, columns)
        if step == 0:
            edge = jnp.dot(lines, table_ref[:, width:], preferred_element_type=jnp.float32)
            edge = edge.reshape(parts * per, FY, MARGIN) * keep_ref[...][None]
            done_ref[0, :, :, :MARGIN] += edge
        for part in range(parts):
            copy(step, part).start()
    for step in range(max(steps - 2, 0), steps):
        for part in range(parts):
            copy(step, part).wait()


def add_image(image, place, pieces, turn, table, keep, total_pols, scale):
    parts, per = len(pieces), pieces[0].shape[0]
    pols = parts * per
    columns = 512
    depth = table.shape[0]
    width = table.shape[1] - MARGIN
    vmem = pl.BlockSpec(memory_space=pltpu.VMEM)
    operands = [*pieces, turn, table, keep]
    in_specs = [vmem] * len(operands)
    aliases = {}
    if image is not None:
        operands.append(image)
        in_specs.append(pl.BlockSpec(memory_space=pl.ANY))
        aliases = {len(operands): 0}
    return pl.pallas_call(
        functools.partial(image_kernel, parts=parts, scale=scale, columns=columns),
        out_shape=jax.ShapeDtypeStruct((total_pols, FY, width), jnp.float32),
        grid_spec=pltpu.PrefetchScalarGridSpec(
            num_scalar_prefetch=1,
            grid=(),
            in_specs=in_specs,
            out_specs=pl.BlockSpec(memory_space=pl.ANY),
            scratch_shapes=[
                pltpu.VMEM((pols * FY, depth), jnp.bfloat16),
                pltpu.VMEM((2, pols, FY, columns), jnp.float32),
                pltpu.SemaphoreType.DMA((2, parts)),
            ],
        ),
        input_output_aliases=aliases,
        compiler_params=pltpu.CompilerParams(vmem_limit_bytes=28 << 20),
        cost_estimate=pl.CostEstimate(
            flops=2 * pols * FY * depth * width,
            bytes_accessed=2 * depth * width + 4 * pols * FY * width,
            transcendentals=0,
        ),
        name="add_image",
    )(place, *operands)


def shards(
    visibilities, w_kernel, w_index, cell_offsets, block_sub, intersection_rows, intersection_count
):
    cores, east = lax.axis_size("core"), lax.axis_size("x")
    north, upper = lax.axis_size("y"), lax.axis_size("z0")
    groups, facets = north * cores, lax.axis_size(FACET)
    num_chans, num_parts, _, row_len = visibilities.shape
    num_pols = num_parts // 2
    own_chans = num_chans // groups
    shares = upper * east
    chan_shares = math.gcd(shares, own_chans)
    pol_shares = shares // chan_shares
    per_chan, per_pol = own_chans // chan_shares, num_pols // pol_shares
    lines = 2 * per_chan * per_pol
    blocks = row_len // BLK
    period = FX * facets
    z0, x = lax.axis_index("z0"), lax.axis_index("x")

    def scalar(value):
        return jnp.reshape(value, (1,)).astype(jnp.int32)

    vis = visibilities.reshape(num_chans, num_parts, row_len)
    sent = pack_rows(
        scalar(lax.axis_index(CHAN)),
        vis,
        w_index,
        cell_offsets,
        block_sub,
        (chan_shares, pol_shares, per_chan, per_pol, cores),
        north * shares,
        lines,
    )
    rows = [
        lax.all_to_all(part, ("y", "z0", "x"), split_axis=0, concat_axis=0, tiled=True)
        for part in sent
    ]
    sub_ids = rows[0][:, 0, -LANES : blocks - LANES].astype(jnp.int32).reshape(-1)
    table, turn, keep = make_tables(
        scalar(lax.axis_index(FACET)), intersection_rows, intersection_count, period
    )
    taps = w_kernel.astype(jnp.float32).transpose(1, 2, 0).reshape(-1, w_kernel.shape[0])
    taps = jnp.pad(taps, ((0, 0), (0, LANES - taps.shape[1])))

    def total(*arrays):
        return sum(a.astype(jnp.float32) for a in arrays).astype(jnp.bfloat16)

    place = scalar(lax.axis_index("core"))
    scale = 1.0 / math.sqrt(groups * facets * row_len)
    image = None
    token = keep
    for half in range(2):
        own, other = grid_rows(place, sub_ids, taps, rows[0], rows[half], row_len, token)
        token = own
        both = total(own, swap(other, "core"))
        mine = total(both, swap(both, "z1"))
        pieces, spots = [], []
        for z_step in range(upper):
            for x_step in range(east):
                route = [
                    (a * east + b, (a + z_step) % upper * east + (b + x_step) % east)
                    for a in range(upper)
                    for b in range(east)
                ]
                piece = lax.ppermute(mine, ("z0", "x"), route) if z_step + x_step else mine
                pieces.append(piece)
                share = lax.rem(z0 + upper - z_step, upper) * east
                share = share + lax.rem(x + east - x_step, east)
                spots.append(share * per_chan * per_pol + half * (per_chan * per_pol // 2))
        spots = jnp.stack(spots).astype(jnp.int32)
        image = add_image(image, spots, pieces, turn, table, keep, own_chans * num_pols, scale)
    return image.reshape(own_chans, num_pols, FY, FX)


def solution(mesh):
    groups, facets = mesh.shape["chan"], mesh.shape["facet"]
    inner = Mesh(
        mesh.devices.reshape(groups // 2, 2, 2, 2, facets // 4), CHAN + FACET
    )
    return jax.shard_map(
        shards,
        mesh=inner,
        in_specs=(
            P(None, None, CHAN, FACET),
            P(),
            P(None, FACET),
            P(None, None, FACET),
            P(None, FACET),
            P(),
            P(),
        ),
        out_specs=P(CHAN, None, None, FACET),
        check_vma=False,
    )
```

```python
import functools
import math

import jax
import jax.numpy as jnp
from jax import lax
from jax.experimental import pallas as pl
from jax.experimental.pallas import tpu as pltpu
from jax.sharding import Mesh
from jax.sharding import PartitionSpec as P

BLK = 512
SG = 32
NSUB = 32
FX = 2048
FY = 64
MARGIN = 128
LANES = 128
PACK = LANES // SG
SETS = NSUB // PACK
CHAN = ("y", "core")
VMEM_LIMIT = 56 << 20
FACET = ("z1", "z0", "x")


def swap(block, axis):
    return lax.ppermute(block, axis, [(0, 1), (1, 0)])


def pack_kernel(
    group_ref, vis_from, plane_from, cell_from, sub_from, first_ref, second_ref, *refs, shares
):
    vis_ref, plane_ref, cell_ref, sub_ref, sems, vis_sems = refs
    chan_shares, pol_shares, per_chan, per_pol, cores = shares
    num_pols = vis_ref.shape[1] // 2
    row_len = vis_ref.shape[2]
    lines = first_ref.shape[1]
    width = row_len // lines
    half = per_pol // 2
    group = group_ref[0]
    small = [(plane_from, plane_ref), (cell_from, cell_ref), (sub_from, sub_ref)]
    small = [pltpu.make_async_copy(*pair, sems.at[k]) for k, pair in enumerate(small)]
    dests = first_ref.shape[0]
    step = vis_ref.shape[0] // (dests // (chan_shares * pol_shares))
    large = []
    for k in range(vis_ref.shape[0] // step):
        chans = pl.ds(k * step, step)
        large.append(
            pltpu.make_async_copy(vis_from.at[chans], vis_ref.at[chans], vis_sems.at[k])
        )
    for copy in small + large:
        copy.start()
    for copy in small:
        copy.wait()

    def folded(row):
        row = row.astype(jnp.float32)
        return jnp.concatenate([row[:, k * width : (k + 1) * width] for k in range(lines)], axis=0)

    subs = sub_ref[pl.ds(group, 1), :].astype(jnp.float32)
    subs = jnp.concatenate([subs, jnp.zeros((1, LANES - subs.shape[1]), jnp.float32)], axis=1)
    ids = [
        folded(plane_ref[pl.ds(group, 1), :]),
        folded(cell_ref[0, pl.ds(group, 1), :]),
        folded(cell_ref[1, pl.ds(group, 1), :]),
        jnp.broadcast_to(subs, (lines, LANES)),
    ]
    ids = jnp.concatenate(ids, axis=1).astype(jnp.bfloat16)
    dest = 0
    for north, copy in enumerate(large):
        copy.wait()
        for chan_share in range(chan_shares):
            for pol_share in range(pol_shares):
                found = ([], [])
                for core in range(cores):
                    chans = (north * cores + core) * chan_shares + chan_share
                    chans = [
                        vis_ref[chans * per_chan + k].astype(jnp.float32) for k in range(per_chan)
                    ]
                    for part in range(2):
                        start = part * num_pols + pol_share * per_pol
                        for vis in chans:
                            found[0].append(vis[start : start + half])
                            found[1].append(vis[start + half : start + per_pol])
                first_ref[dest, :, :row_len] = jnp.concatenate(found[0], 0).astype(jnp.bfloat16)
                first_ref[dest, :, row_len:] = ids
                second_ref[dest] = jnp.concatenate(found[1], 0).astype(jnp.bfloat16)
                dest += 1


def pack_rows(group, vis, planes, cells, subs, shares, dests, lines):
    row_len = vis.shape[2]
    extra = 3 * row_len // lines + LANES
    norths = dests // (shares[0] * shares[1])
    vmem = pl.BlockSpec(memory_space=pltpu.VMEM)
    return pl.pallas_call(
        functools.partial(pack_kernel, shares=shares),
        out_shape=[
            jax.ShapeDtypeStruct((dests, lines, row_len + extra), jnp.bfloat16),
            jax.ShapeDtypeStruct((dests, lines, row_len), jnp.bfloat16),
        ],
        grid_spec=pltpu.PrefetchScalarGridSpec(
            num_scalar_prefetch=1,
            grid=(),
            in_specs=[pl.BlockSpec(memory_space=pl.ANY)] * 4,
            out_specs=[vmem] * 2,
            scratch_shapes=[pltpu.VMEM(a.shape, a.dtype) for a in (vis, planes, cells, subs)]
            + [pltpu.SemaphoreType.DMA((3,)), pltpu.SemaphoreType.DMA((norths,))],
        ),
        compiler_params=pltpu.CompilerParams(vmem_limit_bytes=VMEM_LIMIT),
        cost_estimate=pl.CostEstimate(flops=1 << 20, bytes_accessed=3 << 20, transcendentals=0),
        name="pack_rows",
    )(group, vis, planes, cells, subs)


def grid_kernel(place_ref, sub_ref, taps_ref, ids_ref, rows_ref, *refs, row_len, ids_from):
    own_ref, other_ref, sums_ref = refs[-3:]
    step = pl.program_id(0)
    lines = rows_ref.shape[1]
    pols = lines // 4
    cells = 2 * pols * SG
    blocks = row_len // BLK
    width = row_len // lines

    @pl.when(step == 0)
    def _():
        sums_ref[...] = jnp.zeros_like(sums_ref)

    taps = taps_ref[...]
    ids = ids_ref[0, :, ids_from : ids_from + 3 * width].astype(jnp.float32).astype(jnp.int32)
    cell = lax.broadcasted_iota(jnp.int32, (8, BLK), 0)

    def listed(kind, block):
        found = []
        for start in range(block * BLK, (block + 1) * BLK, min(BLK, width)):
            line, column = start // width, kind * width + start % width
            found.append(ids[line : line + 1, column : column + min(BLK, width)])
        return jnp.concatenate(found, axis=1) if len(found) > 1 else found[0]

    def pick(values, index, axis):
        found = [
            jnp.take_along_axis(
                values if axis else values[:, c : c + LANES], index[:, c : c + LANES], axis=axis
            )
            for c in range(0, BLK, LANES)
        ]
        return jnp.concatenate(found, axis=1)

    def spread(values, offset):
        distance = cell - offset
        keep = [
            (distance + 8 * tile >= 0) & (distance + 8 * tile < 8) for tile in range(SG // 8)
        ]
        turned = [pick(values[8 * q : 8 * q + 8], distance & 7, 0) for q in range(2)]
        return [
            jnp.concatenate([jnp.where(m, part, 0.0) for m in keep], axis=0) for part in turned
        ]

    for block in range(blocks):
        plane = jnp.broadcast_to(listed(0, block), (16, BLK))
        values = pick(taps, plane, 1)
        left = jnp.concatenate(spread(values, listed(1, block)), axis=0).astype(jnp.bfloat16)
        kern_re, kern_im = spread(values, listed(2, block))
        vis = rows_ref[0, :, block * BLK : (block + 1) * BLK].astype(jnp.float32)
        vis = pltpu.roll(vis, place_ref[0] * (lines // 2), 0)
        real, imag = [], []
        for first in (0, 2 * pols):
            for row in range(first, first + pols):
                vis_re = vis[row : row + 1]
                vis_im = vis[row + pols : row + pols + 1]
                real.append((vis_re * kern_re - vis_im * kern_im).astype(jnp.bfloat16))
                imag.append((vis_re * kern_im + vis_im * kern_re).astype(jnp.bfloat16))
        weighted = jnp.concatenate(real + imag, axis=0)
        sub = sub_ref[step * blocks + block]
        sums_ref[sub] += lax.dot_general(
            left, weighted, (((1,), (1,)), ((), ())), preferred_element_type=jnp.float32
        )

    @pl.when(step == pl.num_programs(0) - 1)
    def _():
        slot = lax.broadcasted_iota(jnp.int32, (2 * SG, LANES), 1) // SG

        def finish(group, carry):
            parts = []
            for k in range(PACK):
                raw = sums_ref[group * PACK + k]
                real = raw[:SG, :cells] - raw[SG:, cells:]
                imag = raw[:SG, cells:] + raw[SG:, :cells]
                part = jnp.concatenate([real, imag], axis=0)
                if cells < LANES:
                    part = jnp.concatenate([part, jnp.zeros_like(part)], axis=1)
                parts.append(part)
            for pol in range(2 * pols):
                tile = slice(pol // PACK * LANES, (pol // PACK + 1) * LANES)
                packed = jnp.zeros((2 * SG, LANES), jnp.float32)
                for k in range(PACK):
                    move = (k - pol) % PACK * SG
                    part = parts[k][:, tile]
                    part = pltpu.roll(part, move, 1) if move else part
                    packed = jnp.where(slot == k, part, packed)
                out_ref = own_ref if pol < pols else other_ref
                out_ref[pol % pols, group] = packed.astype(jnp.bfloat16)
            return carry

        lax.fori_loop(0, SETS, finish, 0)


def grid_rows(place, sub_ids, taps, ids, rows, row_len, after):
    sources, lines, _ = rows.shape
    pols = lines // 4
    shape = (pols, SETS, 2 * SG, LANES)
    whole = pl.BlockSpec(shape, lambda s, *_: (0, 0, 0, 0))
    flops = 2 * sources * row_len * 2 * SG * 4 * pols * SG
    return pl.pallas_call(
        functools.partial(grid_kernel, row_len=row_len, ids_from=row_len),
        out_shape=[jax.ShapeDtypeStruct(shape, jnp.bfloat16)] * 2,
        grid_spec=pltpu.PrefetchScalarGridSpec(
            num_scalar_prefetch=2,
            grid=(sources,),
            in_specs=[
                pl.BlockSpec(taps.shape, lambda s, *_: (0, 0)),
                pl.BlockSpec((1,) + ids.shape[1:], lambda s, *_: (s, 0, 0)),
                pl.BlockSpec((1,) + rows.shape[1:], lambda s, *_: (s, 0, 0)),
            ]
            + [pl.BlockSpec(memory_space=pl.ANY)] * len(after),
            out_specs=[whole] * 2,
            scratch_shapes=[pltpu.VMEM((NSUB, 2 * SG, 4 * pols * SG), jnp.float32)],
        ),
        compiler_params=pltpu.CompilerParams(vmem_limit_bytes=16 << 20),
        cost_estimate=pl.CostEstimate(
            flops=flops * 8, bytes_accessed=2 << 20, transcendentals=0
        ),
        name="grid_rows",
    )(place, sub_ids, taps, ids, rows, *after)


def add_kernel(*refs, terms):
    total = refs[0][...].astype(jnp.float32)
    for ref in refs[1:terms]:
        total = total + ref[...].astype(jnp.float32)
    refs[-1][...] = total.astype(jnp.bfloat16)


def add(terms, after=()):
    vmem = pl.BlockSpec(memory_space=pltpu.VMEM)
    return pl.pallas_call(
        functools.partial(add_kernel, terms=len(terms)),
        out_shape=jax.ShapeDtypeStruct(terms[0].shape, jnp.bfloat16),
        in_specs=[vmem] * len(terms) + [pl.BlockSpec(memory_space=pl.ANY)] * len(after),
        out_specs=vmem,
        compiler_params=pltpu.CompilerParams(vmem_limit_bytes=4 << 20),
        cost_estimate=pl.CostEstimate(flops=1 << 18, bytes_accessed=4 << 20, transcendentals=0),
        name="add_sums",
    )(*terms, *after)


def wrapped(value, period):
    if period & (period - 1):
        return jnp.mod(value, period)
    return value & (period - 1)


def circle(phase, period):
    phase = wrapped(phase, period)
    quarter = lax.div(phase + period // 8, period // 4)
    rest = phase - quarter * (period // 4)
    angle = rest.astype(jnp.float32) * (2.0 * math.pi / period)
    square = angle * angle
    sin = -1.0 / 5040 + square * (1.0 / 362880)
    sin = -1.0 / 6 + square * (1.0 / 120 + square * sin)
    sin = angle + angle * square * sin
    cos = -1.0 / 720 + square * (1.0 / 40320)
    cos = 1.0 + square * (-0.5 + square * (1.0 / 24 + square * cos))
    odd = (quarter & 1) == 1
    full_cos, full_sin = jnp.where(odd, sin, cos), jnp.where(odd, cos, sin)
    full_cos = jnp.where(((quarter + 1) & 2) == 2, -full_cos, full_cos)
    return full_cos, jnp.where((quarter & 2) == 2, -full_sin, full_sin)


def tables_kernel(facet_ref, listed_ref, count_ref, *refs, period):
    table_ref, turn_ref, keep_ref = refs[-3:]
    facet = facet_ref[0]
    group = pl.program_id(0)
    span = period // SG
    cells = PACK * SG
    row = lax.broadcasted_iota(jnp.int32, (cells, LANES), 0)
    lane = lax.broadcasted_iota(jnp.int32, (cells, LANES), 1)
    tiles = table_ref.shape[1] // LANES
    start = facet * FX - period // 2 + jnp.where(lane == tiles - 1, -MARGIN, lane * LANES)
    sub = group * PACK + (row >> 5)
    cell = (wrapped(sub * 53 + 5, span) - span // 2) * SG + (row & (SG - 1))
    fine_cos, fine_sin = circle(cell * lane, period)
    coarse_cos, coarse_sin = circle(cell * start, period)
    for tile in range(tiles):
        columns = slice(tile * LANES, (tile + 1) * LANES)
        tile_cos = coarse_cos[:, tile : tile + 1]
        tile_sin = coarse_sin[:, tile : tile + 1]
        full_cos = tile_cos * fine_cos - tile_sin * fine_sin
        full_sin = tile_sin * fine_cos + tile_cos * fine_sin
        table_ref[:cells, columns] = full_cos.astype(jnp.bfloat16)
        table_ref[cells:, columns] = (-full_sin).astype(jnp.bfloat16)

    turn_shape = (2 * FY, 2 * PACK * SG)
    row = lax.broadcasted_iota(jnp.int32, turn_shape, 0)
    lane = lax.broadcasted_iota(jnp.int32, turn_shape, 1)
    sub = group * PACK + (lane >> 6)
    cell = (wrapped(sub * 37, span) - span // 2) * SG + (lane & (SG - 1))
    quarter = (lane >> 5 & 1) - (row >> 6)
    phase = cell * ((row & (FY - 1)) - FY // 2) + quarter * (period // 4)
    turn_ref[0] = circle(phase, period)[0].astype(jnp.bfloat16)

    @pl.when(group == 0)
    def _():
        line = lax.broadcasted_iota(jnp.int32, (FY, MARGIN), 0)
        before = jnp.maximum(facet - 1, 0)
        in_use = jnp.where(facet > 0, count_ref[before], 0)

        def mark(k, keep):
            return jnp.where((line == listed_ref[before, k]) & (k < in_use), 1.0, keep)

        keep_ref[...] = lax.fori_loop(
            0, listed_ref.shape[1], mark, jnp.zeros((FY, MARGIN), jnp.float32)
        )


def make_tables(facet, listed, counts, period, token):
    depth, width = 2 * NSUB * SG, FX + MARGIN
    turn = (1, 2 * FY, 2 * PACK * SG)
    return pl.pallas_call(
        functools.partial(tables_kernel, period=period),
        out_shape=[
            jax.ShapeDtypeStruct((depth, width), jnp.bfloat16),
            jax.ShapeDtypeStruct((SETS,) + turn[1:], jnp.bfloat16),
            jax.ShapeDtypeStruct((FY, MARGIN), jnp.float32),
        ],
        grid_spec=pltpu.PrefetchScalarGridSpec(
            num_scalar_prefetch=3,
            grid=(SETS,),
            in_specs=[pl.BlockSpec(memory_space=pl.ANY)],
            out_specs=[
                pl.BlockSpec((depth // SETS, width), lambda g, *_: (g, 0)),
                pl.BlockSpec(turn, lambda g, *_: (g, 0, 0)),
                pl.BlockSpec((FY, MARGIN), lambda g, *_: (0, 0)),
            ],
        ),
        compiler_params=pltpu.CompilerParams(vmem_limit_bytes=16 << 20),
        cost_estimate=pl.CostEstimate(
            flops=8 * depth * width, bytes_accessed=2 * depth * width, transcendentals=1 << 19
        ),
        name="make_tables",
    )(facet, listed, counts, token)


def image_kernel(place_ref, *refs, parts, scale, columns):
    piece_refs = refs[:parts]
    turn_ref, table_ref, keep_ref = refs[parts : parts + 3]
    out_ref, lines_ref, done_ref, sems = refs[-4:]
    per = piece_refs[0].shape[0]
    width = table_ref.shape[1] - MARGIN
    slot = lax.broadcasted_iota(jnp.int32, (2 * SG, 2 * LANES), 1) % LANES // SG
    flat = [(part, i) for part in range(parts) for i in range(per)]

    def group_rows(group, carry):
        base = pl.multiple_of(group * 2 * LANES, 2 * LANES)
        for k in range(0, len(flat), 2):
            pair = [piece_refs[part][i, group] for part, i in flat[k : k + 2]]
            pair = jnp.concatenate(pair, axis=1)
            zero = jnp.zeros_like(pair)
            spread = [jnp.where(slot == s, pair, zero) for s in range(PACK)]
            spread = jnp.concatenate(spread, axis=0)
            turned = jnp.dot(turn_ref[group], spread, preferred_element_type=jnp.float32)
            turned = (turned * scale).astype(jnp.bfloat16)
            for m in range(2):
                for q in range(2):
                    lines_ref[
                        (k + m) * FY : (k + m + 1) * FY, pl.ds(base + q * LANES, LANES)
                    ] = turned[q * FY : (q + 1) * FY, m * LANES : (m + 1) * LANES]
        return carry

    lax.fori_loop(0, SETS, group_rows, 0)
    lines = lines_ref[...]

    def copy(step, part):
        return pltpu.make_async_copy(
            done_ref.at[step % 2, pl.ds(part * per, per)],
            out_ref.at[pl.ds(place_ref[part], per), :, pl.ds(step * columns, columns)],
            sems.at[step % 2, part],
        )

    steps = width // columns
    for step in range(steps):
        if step >= 2:
            for part in range(parts):
                copy(step - 2, part).wait()
        block = table_ref[:, step * columns : (step + 1) * columns]
        total = jnp.dot(lines, block, preferred_element_type=jnp.float32)
        done_ref[step % 2] = total.reshape(parts * per, FY, columns)
        if step == 0:
            edge = jnp.dot(lines, table_ref[:, width:], preferred_element_type=jnp.float32)
            edge = edge.reshape(parts * per, FY, MARGIN) * keep_ref[...][None]
            done_ref[0, :, :, :MARGIN] += edge
        for part in range(parts):
            copy(step, part).start()
    for step in range(max(steps - 2, 0), steps):
        for part in range(parts):
            copy(step, part).wait()


def add_image(image, place, pieces, turn, table, keep, total_pols, scale, after):
    parts, per = len(pieces), pieces[0].shape[0]
    pols = parts * per
    columns = 512
    depth = table.shape[0]
    width = table.shape[1] - MARGIN
    vmem = pl.BlockSpec(memory_space=pltpu.VMEM)
    operands = [*pieces, turn, table, keep]
    in_specs = [vmem] * len(operands)
    operands.extend(after)
    in_specs.extend([pl.BlockSpec(memory_space=pl.ANY)] * len(after))
    aliases = {}
    if image is not None:
        operands.append(image)
        in_specs.append(pl.BlockSpec(memory_space=pl.ANY))
        aliases = {len(operands): 0}
    return pl.pallas_call(
        functools.partial(image_kernel, parts=parts, scale=scale, columns=columns),
        out_shape=jax.ShapeDtypeStruct((total_pols, FY, width), jnp.float32),
        grid_spec=pltpu.PrefetchScalarGridSpec(
            num_scalar_prefetch=1,
            grid=(),
            in_specs=in_specs,
            out_specs=pl.BlockSpec(memory_space=pl.ANY),
            scratch_shapes=[
                pltpu.VMEM((pols * FY, depth), jnp.bfloat16),
                pltpu.VMEM((2, pols, FY, columns), jnp.float32),
                pltpu.SemaphoreType.DMA((2, parts)),
            ],
        ),
        input_output_aliases=aliases,
        compiler_params=pltpu.CompilerParams(vmem_limit_bytes=28 << 20),
        cost_estimate=pl.CostEstimate(
            flops=2 * pols * FY * depth * width,
            bytes_accessed=2 * depth * width + 4 * pols * FY * width,
            transcendentals=0,
        ),
        name="add_image",
    )(place, *operands)


def shards(
    visibilities, w_kernel, w_index, cell_offsets, block_sub, intersection_rows, intersection_count
):
    cores, east = lax.axis_size("core"), lax.axis_size("x")
    north, upper = lax.axis_size("y"), lax.axis_size("z0")
    groups, facets = north * cores, lax.axis_size(FACET)
    num_chans, num_parts, _, row_len = visibilities.shape
    num_pols = num_parts // 2
    own_chans = num_chans // groups
    shares = upper * east
    chan_shares = math.gcd(shares, own_chans)
    pol_shares = shares // chan_shares
    per_chan, per_pol = own_chans // chan_shares, num_pols // pol_shares
    lines = 2 * per_chan * per_pol
    blocks = row_len // BLK
    period = FX * facets
    z0, x = lax.axis_index("z0"), lax.axis_index("x")

    def scalar(value):
        return jnp.reshape(value, (1,)).astype(jnp.int32)

    vis = visibilities.reshape(num_chans, num_parts, row_len)
    sent = pack_rows(
        scalar(lax.axis_index(CHAN)),
        vis,
        w_index,
        cell_offsets,
        block_sub,
        (chan_shares, pol_shares, per_chan, per_pol, cores),
        north * shares,
        lines,
    )
    rows = [
        lax.all_to_all(part, ("y", "z0", "x"), split_axis=0, concat_axis=0, tiled=True)
        for part in sent
    ]
    sub_ids = rows[0][:, 0, -LANES : blocks - LANES].astype(jnp.int32).reshape(-1)
    taps = w_kernel.astype(jnp.float32).transpose(1, 2, 0).reshape(-1, w_kernel.shape[0])
    taps = jnp.pad(taps, ((0, 0), (0, LANES - taps.shape[1])))

    place = scalar(lax.axis_index("core"))
    scale = 1.0 / math.sqrt(groups * facets * row_len)

    def gridded(half, after):
        own, other = grid_rows(place, sub_ids, taps, rows[0], rows[half], row_len, after)
        return own, swap(other, "core")

    def gathered(mine):
        pieces = [mine]
        for z_step in range(upper):
            for x_step in range(east):
                route = [
                    (a * east + b, (a + z_step) % upper * east + (b + x_step) % east)
                    for a in range(upper)
                    for b in range(east)
                ]
                if z_step + x_step:
                    pieces.append(lax.ppermute(mine, ("z0", "x"), route))
        return pieces

    def spots(half):
        found = []
        for z_step in range(upper):
            for x_step in range(east):
                share = lax.rem(z0 + upper - z_step, upper) * east
                share = share + lax.rem(x + east - x_step, east)
                found.append(share * per_chan * per_pol + half * (per_chan * per_pol // 2))
        return jnp.stack(found).astype(jnp.int32)

    first = add(gridded(0, ()))
    first_far = swap(first, "z1")
    second = gridded(1, (first,))
    first = add((first, first_far), second[:1])
    second = add(second, (first,))
    second_far = swap(second, "z1")
    first_pieces = gathered(first)
    table, turn, keep = make_tables(
        scalar(lax.axis_index(FACET)), intersection_rows, intersection_count, period, first
    )
    second = add((second, second_far))
    second_pieces = gathered(second)
    total_pols = own_chans * num_pols
    image = None
    for half, pieces, after in ((0, first_pieces, (second,)), (1, second_pieces, ())):
        image = add_image(
            image, spots(half), pieces, turn, table, keep, total_pols, scale, after
        )
    return image.reshape(own_chans, num_pols, FY, FX)


def solution(mesh):
    groups, facets = mesh.shape["chan"], mesh.shape["facet"]
    inner = Mesh(
        mesh.devices.reshape(groups // 2, 2, 2, 2, facets // 4), CHAN + FACET
    )
    return jax.shard_map(
        shards,
        mesh=inner,
        in_specs=(
            P(None, None, CHAN, FACET),
            P(),
            P(None, FACET),
            P(None, None, FACET),
            P(None, FACET),
            P(),
            P(),
        ),
        out_specs=P(CHAN, None, None, FACET),
        check_vma=False,
    )
```

```python
import functools
import math

import jax
import jax.numpy as jnp
from jax import lax
from jax.experimental import pallas as pl
from jax.experimental.pallas import tpu as pltpu
from jax.sharding import Mesh
from jax.sharding import PartitionSpec as P

BLK = 512
SG = 32
NSUB = 32
FX = 2048
FY = 64
MARGIN = 128
LANES = 128
PACK = LANES // SG
SETS = NSUB // PACK
CHAN = ("y", "core")
VMEM_LIMIT = 56 << 20
FACET = ("z1", "z0", "x")


def swap(block, axis):
    return lax.ppermute(block, axis, [(0, 1), (1, 0)])


def pack_kernel(
    group_ref, flip_ref, vis_from, plane_from, cell_from, sub_from, first_ref, second_ref, *refs, shares
):
    vis_ref, plane_ref, cell_ref, sub_ref, sems, vis_sems = refs
    chan_shares, pol_shares, per_chan, per_pol, cores, east = shares
    num_pols = vis_ref.shape[1] // 2
    row_len = vis_ref.shape[2]
    lines = first_ref.shape[1]
    width = row_len // lines
    half = per_pol // 2
    group = group_ref[0]
    small = [(plane_from, plane_ref), (cell_from, cell_ref), (sub_from, sub_ref)]
    small = [pltpu.make_async_copy(*pair, sems.at[k]) for k, pair in enumerate(small)]
    dests = first_ref.shape[0]
    step = vis_ref.shape[0] // (dests // (chan_shares * pol_shares))
    large = []
    for k in range(vis_ref.shape[0] // step):
        chans = pl.ds(k * step, step)
        large.append(
            pltpu.make_async_copy(vis_from.at[chans], vis_ref.at[chans], vis_sems.at[k])
        )
    for copy in small + large:
        copy.start()
    for copy in small:
        copy.wait()

    def folded(row):
        row = row.astype(jnp.float32)
        return jnp.concatenate([row[:, k * width : (k + 1) * width] for k in range(lines)], axis=0)

    subs = sub_ref[pl.ds(group, 1), :].astype(jnp.float32)
    subs = jnp.concatenate([subs, jnp.zeros((1, LANES - subs.shape[1]), jnp.float32)], axis=1)
    ids = [
        folded(plane_ref[pl.ds(group, 1), :]),
        folded(cell_ref[0, pl.ds(group, 1), :]),
        folded(cell_ref[1, pl.ds(group, 1), :]),
        jnp.broadcast_to(subs, (lines, LANES)),
    ]
    ids = jnp.concatenate(ids, axis=1).astype(jnp.bfloat16)
    def fill(flip):
        for north, copy in enumerate(large):
            copy.wait()
            for chan_share in range(chan_shares):
                for pol_share in range(pol_shares):
                    found = ([], [])
                    share = chan_share * pol_shares + pol_share
                    dest = north * chan_shares * pol_shares
                    dest = dest + (share // east + flip) % 2 * east + share % east
                    for core in range(cores):
                        chans = (north * cores + core) * chan_shares + chan_share
                        chans = [
                            vis_ref[chans * per_chan + k].astype(jnp.float32) for k in range(per_chan)
                        ]
                        for part in range(2):
                            start = part * num_pols + pol_share * per_pol
                            for vis in chans:
                                found[0].append(vis[start : start + half])
                                found[1].append(vis[start + half : start + per_pol])
                    first_ref[dest, :, :row_len] = jnp.concatenate(found[0], 0).astype(jnp.bfloat16)
                    first_ref[dest, :, row_len:] = ids
                    second_ref[dest] = jnp.concatenate(found[1], 0).astype(jnp.bfloat16)

    for flip in range(2):
        pl.when(flip_ref[0] == flip)(functools.partial(fill, flip))


def pack_rows(group, flip, vis, planes, cells, subs, shares, dests, lines):
    row_len = vis.shape[2]
    extra = 3 * row_len // lines + LANES
    norths = dests // (shares[0] * shares[1])
    vmem = pl.BlockSpec(memory_space=pltpu.VMEM)
    return pl.pallas_call(
        functools.partial(pack_kernel, shares=shares),
        out_shape=[
            jax.ShapeDtypeStruct((dests, lines, row_len + extra), jnp.bfloat16),
            jax.ShapeDtypeStruct((dests, lines, row_len), jnp.bfloat16),
        ],
        grid_spec=pltpu.PrefetchScalarGridSpec(
            num_scalar_prefetch=2,
            grid=(),
            in_specs=[pl.BlockSpec(memory_space=pl.ANY)] * 4,
            out_specs=[vmem] * 2,
            scratch_shapes=[pltpu.VMEM(a.shape, a.dtype) for a in (vis, planes, cells, subs)]
            + [pltpu.SemaphoreType.DMA((3,)), pltpu.SemaphoreType.DMA((norths,))],
        ),
        compiler_params=pltpu.CompilerParams(vmem_limit_bytes=VMEM_LIMIT),
        cost_estimate=pl.CostEstimate(flops=1 << 20, bytes_accessed=3 << 20, transcendentals=0),
        name="pack_rows",
    )(group, flip, vis, planes, cells, subs)


def grid_kernel(place_ref, taps_ref, ids_ref, rows_ref, *refs, row_len, ids_from):
    own_ref, other_ref, sums_ref, listed_ref, sub_ref, sem = refs[-6:]
    sources, lines = rows_ref.shape[:2]
    pols = lines // 4
    cells = 2 * pols * SG
    blocks = row_len // BLK
    width = row_len // lines

    for source in range(sources):
        subs = ids_ref[source, :, ids_from + 3 * width :].astype(jnp.float32)
        listed_ref[source : source + 1] = subs[:1].astype(jnp.int32)
    copy = pltpu.make_async_copy(listed_ref, sub_ref, sem)
    copy.start()
    sums_ref[...] = jnp.zeros_like(sums_ref)
    copy.wait()
    taps = taps_ref[...].astype(jnp.float32)
    taps = jnp.concatenate([taps, jnp.zeros((16, LANES - taps.shape[1]), jnp.float32)], axis=1)
    cell = lax.broadcasted_iota(jnp.int32, (8, BLK), 0)

    def listed(ids, kind, block):
        found = []
        for start in range(block * BLK, (block + 1) * BLK, min(BLK, width)):
            line, column = start // width, kind * width + start % width
            found.append(ids[line : line + 1, column : column + min(BLK, width)])
        return jnp.concatenate(found, axis=1) if len(found) > 1 else found[0]

    def pick(values, index, axis):
        found = [
            jnp.take_along_axis(
                values if axis else values[:, c : c + LANES], index[:, c : c + LANES], axis=axis
            )
            for c in range(0, BLK, LANES)
        ]
        return jnp.concatenate(found, axis=1)

    level = -(lax.broadcasted_iota(jnp.int32, (16, BLK), 0) >> 3)
    levels = [(level - 2 * k).astype(jnp.float32).astype(jnp.bfloat16) for k in range(SG // 16)]
    none = jnp.zeros((16, BLK), jnp.bfloat16)

    def doubled(part):
        return jnp.concatenate([part, part], axis=0).astype(jnp.bfloat16)

    def turned(values, offset):
        distance = cell - offset
        height = doubled((distance >> 3).astype(jnp.float32))
        parts = [pick(values[8 * q : 8 * q + 8], distance & 7, 0) for q in range(2)]
        return parts, [height == level for level in levels]

    def spread(part, masks):
        part = doubled(part)
        return jnp.concatenate([jnp.where(mask, part, none) for mask in masks], axis=0)

    def grid_source(source):
        ids = ids_ref[source, :, ids_from : ids_from + 3 * width]
        ids = ids.astype(jnp.float32).astype(jnp.int32)
        for block in range(blocks):
            plane = jnp.broadcast_to(listed(ids, 0, block), (16, BLK))
            values = pick(taps, plane, 1)
            parts, masks = turned(values, listed(ids, 1, block))
            left = jnp.concatenate([spread(part, masks) for part in parts], axis=0)
            (kern_re, kern_im), masks = turned(values, listed(ids, 2, block))
            vis = rows_ref[source, :, block * BLK : (block + 1) * BLK].astype(jnp.float32)
            vis = pltpu.roll(vis, place_ref[0] * (lines // 2), 0)
            real, imag = [], []
            for first in (0, 2 * pols):
                for row in range(first, first + pols):
                    vis_re = vis[row : row + 1]
                    vis_im = vis[row + pols : row + pols + 1]
                    real.append(spread(vis_re * kern_re - vis_im * kern_im, masks))
                    imag.append(spread(vis_re * kern_im + vis_im * kern_re, masks))
            weighted = jnp.concatenate(real + imag, axis=0)
            sub = sub_ref[source, block]
            sums_ref[sub] += lax.dot_general(
                left, weighted, (((1,), (1,)), ((), ())), preferred_element_type=jnp.float32
            )

    def grid_sources(step, carry):
        for k in range(unroll):
            grid_source(step * unroll + k)
        return carry

    unroll = math.gcd(sources, 4)
    lax.fori_loop(0, sources // unroll, grid_sources, 0)
    slot = lax.broadcasted_iota(jnp.int32, (2 * SG, LANES), 1) // SG

    def finish(group):
        parts = []
        for k in range(PACK):
            raw = sums_ref[group * PACK + k]
            real = raw[:SG, :cells] - raw[SG:, cells:]
            imag = raw[:SG, cells:] + raw[SG:, :cells]
            part = jnp.concatenate([real, imag], axis=0)
            if cells < LANES:
                part = jnp.concatenate([part, jnp.zeros_like(part)], axis=1)
            parts.append(part)
        for pol in range(2 * pols):
            tile = slice(pol // PACK * LANES, (pol // PACK + 1) * LANES)
            packed = jnp.zeros((2 * SG, LANES), jnp.float32)
            for k in range(PACK):
                move = (k - pol) % PACK * SG
                part = parts[k][:, tile]
                part = pltpu.roll(part, move, 1) if move else part
                packed = jnp.where(slot == k, part, packed)
            out_ref = own_ref if pol < pols else other_ref
            out_ref[pol % pols, group] = packed.astype(jnp.bfloat16)

    for group in range(SETS):
        finish(group)


def grid_rows(place, taps, ids, rows, row_len, after):
    sources, lines, _ = rows.shape
    pols = lines // 4
    shape = (pols, SETS, 2 * SG, LANES)
    vmem = pl.BlockSpec(memory_space=pltpu.VMEM)
    flops = 2 * sources * row_len * 2 * SG * 4 * pols * SG
    return pl.pallas_call(
        functools.partial(grid_kernel, row_len=row_len, ids_from=row_len),
        out_shape=[jax.ShapeDtypeStruct(shape, jnp.bfloat16)] * 2,
        grid_spec=pltpu.PrefetchScalarGridSpec(
            num_scalar_prefetch=1,
            grid=(),
            in_specs=[vmem] * 3 + [pl.BlockSpec(memory_space=pl.ANY)] * len(after),
            out_specs=[vmem] * 2,
            scratch_shapes=[
                pltpu.VMEM((NSUB, 2 * SG, 4 * pols * SG), jnp.float32),
                pltpu.VMEM((sources, LANES), jnp.int32),
                pltpu.SMEM((sources, LANES), jnp.int32),
                pltpu.SemaphoreType.DMA(()),
            ],
        ),
        compiler_params=pltpu.CompilerParams(vmem_limit_bytes=16 << 20),
        cost_estimate=pl.CostEstimate(
            flops=flops * 8, bytes_accessed=2 << 20, transcendentals=0
        ),
        name="grid_rows",
    )(place, taps, ids, rows, *after)


def add_kernel(*refs, terms):
    total = refs[0][...].astype(jnp.float32)
    for ref in refs[1:terms]:
        total = total + ref[...].astype(jnp.float32)
    refs[-1][...] = total.astype(jnp.bfloat16)


def add(terms, after=()):
    vmem = pl.BlockSpec(memory_space=pltpu.VMEM)
    return pl.pallas_call(
        functools.partial(add_kernel, terms=len(terms)),
        out_shape=jax.ShapeDtypeStruct(terms[0].shape, jnp.bfloat16),
        in_specs=[vmem] * len(terms) + [pl.BlockSpec(memory_space=pl.ANY)] * len(after),
        out_specs=vmem,
        compiler_params=pltpu.CompilerParams(vmem_limit_bytes=4 << 20),
        cost_estimate=pl.CostEstimate(flops=1 << 18, bytes_accessed=4 << 20, transcendentals=0),
        name="add_sums",
    )(*terms, *after)


def wrapped(value, period):
    if period & (period - 1):
        return jnp.mod(value, period)
    return value & (period - 1)


def circle(phase, period):
    phase = wrapped(phase, period)
    quarter = lax.div(phase + period // 8, period // 4)
    rest = phase - quarter * (period // 4)
    angle = rest.astype(jnp.float32) * (2.0 * math.pi / period)
    square = angle * angle
    sin = -1.0 / 5040 + square * (1.0 / 362880)
    sin = -1.0 / 6 + square * (1.0 / 120 + square * sin)
    sin = angle + angle * square * sin
    cos = -1.0 / 720 + square * (1.0 / 40320)
    cos = 1.0 + square * (-0.5 + square * (1.0 / 24 + square * cos))
    odd = (quarter & 1) == 1
    full_cos, full_sin = jnp.where(odd, sin, cos), jnp.where(odd, cos, sin)
    full_cos = jnp.where(((quarter + 1) & 2) == 2, -full_cos, full_cos)
    return full_cos, jnp.where((quarter & 2) == 2, -full_sin, full_sin)


def tables_kernel(facet_ref, listed_ref, count_ref, *refs, period):
    table_ref, turn_ref, keep_ref = refs[-3:]
    facet = facet_ref[0]
    span = period // SG
    cells = PACK * SG
    row = lax.broadcasted_iota(jnp.int32, (cells, LANES), 0)
    lane = lax.broadcasted_iota(jnp.int32, (cells, LANES), 1)
    tiles = table_ref.shape[1] // LANES
    room = LANES // PACK
    turn_shape = (FY, 2 * PACK * SG)
    turn_line = lax.broadcasted_iota(jnp.int32, turn_shape, 0) - FY // 2
    turn_lane = lax.broadcasted_iota(jnp.int32, turn_shape, 1)
    second = (turn_lane >> 5 & 1) == 1

    def col_cell(group):
        sub = group * PACK + (row >> 5)
        return (wrapped(sub * 53 + 5, span) - span // 2) * SG + (row & (SG - 1))

    tile_id = lane & (room - 1)
    start = jnp.where(tile_id == tiles - 1, -MARGIN, tile_id * LANES)
    start = facet * FX - period // 2 + start
    for batch in range(SETS // PACK):
        coarse_cos, coarse_sin = circle(col_cell(batch * PACK + (lane >> 5)) * start, period)
        for k in range(PACK):
            group = batch * PACK + k
            base = group * 2 * cells
            fine_cos, fine_sin = circle(col_cell(group) * lane, period)
            for tile in range(tiles):
                columns = slice(tile * LANES, (tile + 1) * LANES)
                at = k * room + tile
                tile_cos = coarse_cos[:, at : at + 1]
                tile_neg = -coarse_sin[:, at : at + 1]
                full_cos = tile_cos * fine_cos + tile_neg * fine_sin
                full_neg = tile_neg * fine_cos - tile_cos * fine_sin
                table_ref[base : base + cells, columns] = full_cos.astype(jnp.bfloat16)
                table_ref[base + cells : base + 2 * cells, columns] = full_neg.astype(
                    jnp.bfloat16
                )

            sub = group * PACK + (turn_lane >> 6)
            cell = (wrapped(sub * 37, span) - span // 2) * SG + (turn_lane & (SG - 1))
            cos, sin = circle(cell * turn_line, period)
            turn_ref[group, :FY] = jnp.where(second, -sin, cos).astype(jnp.bfloat16)
            turn_ref[group, FY:] = jnp.where(second, cos, sin).astype(jnp.bfloat16)

    line = lax.broadcasted_iota(jnp.int32, (FY, MARGIN), 0)
    before = jnp.maximum(facet - 1, 0)
    in_use = jnp.where(facet > 0, count_ref[before], 0)

    def mark(k, keep):
        return jnp.where((line == listed_ref[before, k]) & (k < in_use), 1.0, keep)

    keep_ref[...] = lax.fori_loop(
        0, listed_ref.shape[1], mark, jnp.zeros((FY, MARGIN), jnp.float32)
    )


def make_tables(facet, listed, counts, period, token):
    depth, width = 2 * NSUB * SG, FX + MARGIN
    vmem = pl.BlockSpec(memory_space=pltpu.VMEM)
    return pl.pallas_call(
        functools.partial(tables_kernel, period=period),
        out_shape=[
            jax.ShapeDtypeStruct((depth, width), jnp.bfloat16),
            jax.ShapeDtypeStruct((SETS, 2 * FY, 2 * PACK * SG), jnp.bfloat16),
            jax.ShapeDtypeStruct((FY, MARGIN), jnp.float32),
        ],
        grid_spec=pltpu.PrefetchScalarGridSpec(
            num_scalar_prefetch=3,
            grid=(),
            in_specs=[pl.BlockSpec(memory_space=pl.ANY)],
            out_specs=[vmem] * 3,
        ),
        compiler_params=pltpu.CompilerParams(vmem_limit_bytes=16 << 20),
        cost_estimate=pl.CostEstimate(
            flops=8 * depth * width, bytes_accessed=2 * depth * width, transcendentals=1 << 19
        ),
        name="make_tables",
    )(facet, listed, counts, token)


def image_kernel(z1_ref, z0_ref, x_ref, *refs, places, scale, columns):
    parts = len(places)
    piece_refs = refs[:parts]
    turn_ref, table_ref, keep_ref = refs[parts : parts + 3]
    out_ref, lines_ref, done_ref, sems = refs[-4:]
    per = piece_refs[0].shape[0]
    width = table_ref.shape[1] - MARGIN
    slot = lax.broadcasted_iota(jnp.int32, (2 * SG, 2 * LANES), 1) % LANES // SG
    flat = [(part, i) for part in range(parts) for i in range(per)]

    def group_rows(group):
        base = group * 2 * LANES
        for k in range(0, len(flat), 2):
            pair = [piece_refs[part][i, group] for part, i in flat[k : k + 2]]
            pair = jnp.concatenate(pair, axis=1)
            zero = jnp.zeros_like(pair)
            spread = [jnp.where(slot[:, : pair.shape[1]] == s, pair, zero) for s in range(PACK)]
            spread = jnp.concatenate(spread, axis=0)
            turned = jnp.dot(turn_ref[group], spread, preferred_element_type=jnp.float32)
            turned = (turned * scale).astype(jnp.bfloat16)
            for m in range(pair.shape[1] // LANES):
                for q in range(2):
                    lines_ref[
                        (k + m) * FY : (k + m + 1) * FY, base + q * LANES : base + (q + 1) * LANES
                    ] = turned[q * FY : (q + 1) * FY, m * LANES : (m + 1) * LANES]

    for group in range(SETS):
        group_rows(group)
    lines = lines_ref[...]

    def spot(part):
        z_step, x_step, east, half = places[part]
        share = lax.rem(z0_ref[0] + z1_ref[0] + z_step, 2) * east
        share = share + lax.rem(x_ref[0] + east - x_step, east)
        return (share * 2 + half) * per

    def copy(step, part):
        return pltpu.make_async_copy(
            done_ref.at[step % 2, pl.ds(part * per, per)],
            out_ref.at[pl.ds(spot(part), per), :, pl.ds(step * columns, columns)],
            sems.at[step % 2, part],
        )

    steps = width // columns
    for step in range(steps):
        if step >= 2:
            for part in range(parts):
                copy(step - 2, part).wait()
        block = table_ref[:, step * columns : (step + 1) * columns]
        total = jnp.dot(lines, block, preferred_element_type=jnp.float32)
        done_ref[step % 2] = total.reshape(parts * per, FY, columns)
        if step == 0:
            edge = jnp.dot(lines, table_ref[:, width:], preferred_element_type=jnp.float32)
            edge = edge.reshape(parts * per, FY, MARGIN) * keep_ref[...][None]
            done_ref[0, :, :, :MARGIN] += edge
        for part in range(parts):
            copy(step, part).start()
    for step in range(max(steps - 2, 0), steps):
        for part in range(parts):
            copy(step, part).wait()


def add_image(image, device, places, pieces, turn, table, keep, total_pols, scale, after):
    parts, per = len(pieces), pieces[0].shape[0]
    pols = parts * per
    columns = 1024
    depth = table.shape[0]
    width = table.shape[1] - MARGIN
    vmem = pl.BlockSpec(memory_space=pltpu.VMEM)
    operands = [*pieces, turn, table, keep]
    in_specs = [vmem] * len(operands)
    operands.extend(after)
    in_specs.extend([pl.BlockSpec(memory_space=pl.ANY)] * len(after))
    aliases = {}
    if image is not None:
        operands.append(image)
        in_specs.append(pl.BlockSpec(memory_space=pl.ANY))
        aliases = {len(operands) + 2: 0}
    return pl.pallas_call(
        functools.partial(image_kernel, places=places, scale=scale, columns=columns),
        out_shape=jax.ShapeDtypeStruct((total_pols, FY, width), jnp.float32),
        grid_spec=pltpu.PrefetchScalarGridSpec(
            num_scalar_prefetch=3,
            grid=(),
            in_specs=in_specs,
            out_specs=pl.BlockSpec(memory_space=pl.ANY),
            scratch_shapes=[
                pltpu.VMEM((pols * FY, depth), jnp.bfloat16),
                pltpu.VMEM((2, pols, FY, columns), jnp.float32),
                pltpu.SemaphoreType.DMA((2, parts)),
            ],
        ),
        input_output_aliases=aliases,
        compiler_params=pltpu.CompilerParams(vmem_limit_bytes=28 << 20),
        cost_estimate=pl.CostEstimate(
            flops=2 * pols * FY * depth * width,
            bytes_accessed=2 * depth * width + 4 * pols * FY * width,
            transcendentals=0,
        ),
        name="add_image",
    )(*device, *operands)


def shards(
    visibilities, w_kernel, w_index, cell_offsets, block_sub, intersection_rows, intersection_count
):
    cores, east = lax.axis_size("core"), lax.axis_size("x")
    north, upper = lax.axis_size("y"), lax.axis_size("z0")
    groups, facets = north * cores, lax.axis_size(FACET)
    num_chans, num_parts, _, row_len = visibilities.shape
    num_pols = num_parts // 2
    own_chans = num_chans // groups
    shares = upper * east
    chan_shares = math.gcd(shares, own_chans)
    pol_shares = shares // chan_shares
    per_chan, per_pol = own_chans // chan_shares, num_pols // pol_shares
    lines = 2 * per_chan * per_pol
    period = FX * facets
    z1, z0, x = (lax.axis_index(axis) for axis in ("z1", "z0", "x"))

    def scalar(value):
        return jnp.reshape(value, (1,)).astype(jnp.int32)

    vis = visibilities.reshape(num_chans, num_parts, row_len)
    sent = pack_rows(
        scalar(lax.axis_index(CHAN)),
        scalar(z1),
        vis,
        w_index,
        cell_offsets,
        block_sub,
        (chan_shares, pol_shares, per_chan, per_pol, cores, east),
        north * shares,
        lines,
    )
    rows = [
        lax.all_to_all(part, ("y", "z0", "x"), split_axis=0, concat_axis=0, tiled=True)
        for part in sent
    ]
    taps = w_kernel.transpose(1, 2, 0).reshape(-1, w_kernel.shape[0])
    place = scalar(lax.axis_index("core"))
    scale = 1.0 / math.sqrt(groups * facets * row_len)

    def gridded(half, after):
        own, other = grid_rows(place, taps, rows[0], rows[half], row_len, after)
        return own, swap(other, "core")

    def shifted(piece, z_step, x_step):
        if z_step + x_step == 0:
            return piece
        route = [
            (a * east + b, (a + z_step) % upper * east + (b + x_step) % east)
            for a in range(upper)
            for b in range(east)
        ]
        return lax.ppermute(piece, ("z0", "x"), route)

    def gathered(mine, relay):
        pieces = []
        for z_step in range(upper):
            here = shifted(mine, z_step, 0)
            for x_step in range(east):
                if relay or z_step + x_step == 0:
                    pieces.append(shifted(here, 0, x_step))
                else:
                    pieces.append(shifted(mine, z_step, x_step))
        return pieces

    def mirrored(block):
        return lax.ppermute(block, ("z1", "z0"), [(i, 3 - i) for i in range(4)])

    first = add(gridded(0, ()))
    first_far = mirrored(first)
    second = gridded(1, (first,))
    first = add((first, first_far), second[:1])
    second = add(second, (first,))
    second_far = mirrored(second)
    first_pieces = gathered(first, False)
    table, turn, keep = make_tables(
        scalar(lax.axis_index(FACET)), intersection_rows, intersection_count, period, first
    )
    second = add((second, second_far))
    second_pieces = gathered(second, False)
    total_pols = own_chans * num_pols
    device = [scalar(lax.axis_index(axis)) for axis in ("z1", "z0", "x")]
    places = [
        [(a, b, east, half) for a in range(upper) for b in range(east)] for half in range(2)
    ]
    pieces = first_pieces + second_pieces
    places = places[0] + places[1]
    parts = len(first_pieces)
    image = None
    cuts = (0, parts + 1, 2 * parts - 1, 2 * parts)
    for begin, end in zip(cuts, cuts[1:]):
        image = add_image(
            image,
            device,
            places[begin:end],
            pieces[begin:end],
            turn,
            table,
            keep,
            total_pols,
            scale,
            () if begin else (second,),
        )
    return image.reshape(own_chans, num_pols, FY, FX)


def solution(mesh):
    groups, facets = mesh.shape["chan"], mesh.shape["facet"]
    inner = Mesh(
        mesh.devices.reshape(groups // 2, 2, 2, 2, facets // 4), CHAN + FACET
    )
    return jax.shard_map(
        shards,
        mesh=inner,
        in_specs=(
            P(None, None, CHAN, FACET),
            P(),
            P(None, FACET),
            P(None, None, FACET),
            P(None, FACET),
            P(),
            P(),
        ),
        out_specs=P(CHAN, None, None, FACET),
        check_vma=False,
    )
```

```python
import functools
import math

import jax
import jax.numpy as jnp
from jax import lax
from jax.experimental import pallas as pl
from jax.experimental.pallas import tpu as pltpu
from jax.sharding import Mesh
from jax.sharding import PartitionSpec as P

BLK = 512
SG = 32
NSUB = 32
FX = 2048
FY = 64
MARGIN = 128
LANES = 128
PACK = LANES // SG
SETS = NSUB // PACK
CHAN = ("y", "core")
VMEM_LIMIT = 56 << 20
LATE = (4, 5, 6, 7)
FACET = ("z1", "z0", "x")


def swap(block, axis):
    return lax.ppermute(block, axis, [(0, 1), (1, 0)])


def pack_kernel(
    group_ref, first_ref, flip_ref, vis_from, plane_from, cell_from, sub_from, *refs, shares
):
    out_refs = refs[:-6]
    vis_ref, plane_ref, cell_ref, sub_ref, sems, vis_sem = refs[-6:]
    chan_shares, pol_shares, per_chan, per_pol, cores, east = shares
    all_shares = chan_shares * pol_shares
    num_pols = vis_ref.shape[1] // 2
    row_len = vis_ref.shape[2]
    dests, lines = out_refs[0].shape[0] * len(out_refs), out_refs[0].shape[1]
    width = row_len // lines
    half = per_pol // 2
    group = group_ref[0]
    small = [(plane_from, plane_ref), (cell_from, cell_ref), (sub_from, sub_ref)]
    small = [pltpu.make_async_copy(*pair, sems.at[k]) for k, pair in enumerate(small)]
    large = pltpu.make_async_copy(vis_from, vis_ref, vis_sem)
    for copy in [large] + small:
        copy.start()
    for copy in small:
        copy.wait()

    def folded(row):
        row = row.astype(jnp.float32)
        return jnp.concatenate([row[:, k * width : (k + 1) * width] for k in range(lines)], axis=0)

    subs = sub_ref[pl.ds(group, 1), :].astype(jnp.float32)
    subs = jnp.concatenate([subs, jnp.zeros((1, LANES - subs.shape[1]), jnp.float32)], axis=1)
    ids = [
        folded(plane_ref[pl.ds(group, 1), :]),
        folded(cell_ref[0, pl.ds(group, 1), :]),
        folded(cell_ref[1, pl.ds(group, 1), :]),
        jnp.broadcast_to(subs, (lines, LANES)),
    ]
    ids = jnp.concatenate(ids, axis=1).astype(jnp.bfloat16)
    large.wait()
    for k in range(dests):
        dest = first_ref[0] ^ k if len(out_refs) > 1 else k
        north, share = lax.div(dest, all_shares), lax.rem(dest, all_shares)
        share = lax.rem(lax.div(share, east) + flip_ref[0], 2) * east + lax.rem(share, east)
        chan_share, pol_share = lax.div(share, pol_shares), lax.rem(share, pol_shares)
        found = ([], [])
        for core in range(cores):
            chan = ((north * cores + core) * chan_shares + chan_share) * per_chan
            chans = [vis_ref[chan + i].astype(jnp.float32) for i in range(per_chan)]
            for part in range(2):
                for vis in chans:
                    rows = vis[part * num_pols : part * num_pols + per_pol]
                    for other in range(1, pol_shares):
                        start = part * num_pols + other * per_pol
                        rows = jnp.where(pol_share == other, vis[start : start + per_pol], rows)
                    found[0].append(rows[:half])
                    found[1].append(rows[half:])
        ref, slot = (out_refs[k], 0) if len(out_refs) > 1 else (out_refs[0], k)
        ref[slot, :, :row_len] = jnp.concatenate(found[0], 0).astype(jnp.bfloat16)
        ref[slot, :, row_len : 2 * row_len] = jnp.concatenate(found[1], 0).astype(jnp.bfloat16)
        ref[slot, :, 2 * row_len :] = ids


def pack_rows(device, vis, planes, cells, subs, shares, dests, lines, apart):
    row_len = vis.shape[2]
    width = 2 * row_len + 3 * row_len // lines + LANES
    count = dests if apart else 1
    vmem = pl.BlockSpec(memory_space=pltpu.VMEM)
    return pl.pallas_call(
        functools.partial(pack_kernel, shares=shares),
        out_shape=[jax.ShapeDtypeStruct((dests // count, lines, width), jnp.bfloat16)] * count,
        grid_spec=pltpu.PrefetchScalarGridSpec(
            num_scalar_prefetch=3,
            grid=(),
            in_specs=[pl.BlockSpec(memory_space=pl.ANY)] * 4,
            out_specs=[vmem] * count,
            scratch_shapes=[pltpu.VMEM(a.shape, a.dtype) for a in (vis, planes, cells, subs)]
            + [pltpu.SemaphoreType.DMA((3,)), pltpu.SemaphoreType.DMA(())],
        ),
        compiler_params=pltpu.CompilerParams(vmem_limit_bytes=VMEM_LIMIT),
        cost_estimate=pl.CostEstimate(flops=1 << 20, bytes_accessed=3 << 20, transcendentals=0),
        name="pack_rows",
    )(*device, vis, planes, cells, subs)


def grid_kernel(place_ref, taps_ref, *refs, row_len, half, parts, begins, ends):
    rows_refs = refs[:parts]
    sums_ref, listed_ref, sub_ref, sem = refs[-4:]
    each, lines = rows_refs[0].shape[:2]
    sources = parts * each
    pols = lines // 4
    cells = 2 * pols * SG
    blocks = row_len // BLK
    width = row_len // lines

    ids_from = 2 * row_len
    for source in range(sources):
        subs = rows_refs[source // each][source % each, :, ids_from + 3 * width :]
        subs = subs.astype(jnp.float32)
        listed_ref[source : source + 1] = subs[:1].astype(jnp.int32)
    copy = pltpu.make_async_copy(listed_ref, sub_ref, sem)
    copy.start()
    sums_ref[...] = jnp.zeros_like(sums_ref) if begins else refs[parts][...]
    copy.wait()
    taps = taps_ref[...].astype(jnp.float32)
    taps = jnp.concatenate([taps, jnp.zeros((16, LANES - taps.shape[1]), jnp.float32)], axis=1)
    cell = lax.broadcasted_iota(jnp.int32, (8, BLK), 0)

    def listed(ids, kind, block):
        found = []
        for start in range(block * BLK, (block + 1) * BLK, min(BLK, width)):
            line, column = start // width, kind * width + start % width
            found.append(ids[line : line + 1, column : column + min(BLK, width)])
        return jnp.concatenate(found, axis=1) if len(found) > 1 else found[0]

    def pick(values, index, axis):
        found = [
            jnp.take_along_axis(
                values if axis else values[:, c : c + LANES], index[:, c : c + LANES], axis=axis
            )
            for c in range(0, BLK, LANES)
        ]
        return jnp.concatenate(found, axis=1)

    level = -(lax.broadcasted_iota(jnp.int32, (16, BLK), 0) >> 3)
    levels = [(level - 2 * k).astype(jnp.float32).astype(jnp.bfloat16) for k in range(SG // 16)]
    none = jnp.zeros((16, BLK), jnp.bfloat16)

    def doubled(part):
        return jnp.concatenate([part, part], axis=0).astype(jnp.bfloat16)

    def turned(values, offset):
        distance = cell - offset
        height = doubled((distance >> 3).astype(jnp.float32))
        parts = [pick(values[8 * q : 8 * q + 8], distance & 7, 0) for q in range(2)]
        return parts, [height == level for level in levels]

    def spread(part, masks):
        part = doubled(part)
        return jnp.concatenate([jnp.where(mask, part, none) for mask in masks], axis=0)

    def grid_source(rows_ref, slot, source):
        ids = rows_ref[slot, :, ids_from : ids_from + 3 * width]
        ids = ids.astype(jnp.float32).astype(jnp.int32)
        for block in range(blocks):
            plane = jnp.broadcast_to(listed(ids, 0, block), (16, BLK))
            values = pick(taps, plane, 1)
            parts, masks = turned(values, listed(ids, 1, block))
            left = jnp.concatenate([spread(part, masks) for part in parts], axis=0)
            (kern_re, kern_im), masks = turned(values, listed(ids, 2, block))
            start = half * row_len + block * BLK
            vis = rows_ref[slot, :, start : start + BLK].astype(jnp.float32)
            vis = pltpu.roll(vis, place_ref[0] * (lines // 2), 0)
            real, imag = [], []
            for first in (0, 2 * pols):
                for row in range(first, first + pols):
                    vis_re = vis[row : row + 1]
                    vis_im = vis[row + pols : row + pols + 1]
                    real.append(spread(vis_re * kern_re - vis_im * kern_im, masks))
                    imag.append(spread(vis_re * kern_im + vis_im * kern_re, masks))
            weighted = jnp.concatenate(real + imag, axis=0)
            sub = sub_ref[source, block]
            sums_ref[sub] += lax.dot_general(
                left, weighted, (((1,), (1,)), ((), ())), preferred_element_type=jnp.float32
            )

    unroll = math.gcd(each, 4)

    def grid_sources(step, carry):
        for k in range(unroll):
            slot = step * unroll + k
            grid_source(rows_refs[0], slot, slot)
        return carry

    if parts > 1:
        for source in range(sources):
            grid_source(rows_refs[source // each], source % each, source)
    else:
        lax.fori_loop(0, each // unroll, grid_sources, 0)
    if not ends:
        refs[-5][...] = sums_ref[...]
        return
    own_ref, other_ref = refs[-6:-4]
    slot = lax.broadcasted_iota(jnp.int32, (2 * SG, LANES), 1) // SG

    def finish(group):
        parts = []
        for k in range(PACK):
            raw = sums_ref[group * PACK + k]
            real = raw[:SG, :cells] - raw[SG:, cells:]
            imag = raw[:SG, cells:] + raw[SG:, :cells]
            part = jnp.concatenate([real, imag], axis=0)
            if cells < LANES:
                part = jnp.concatenate([part, jnp.zeros_like(part)], axis=1)
            parts.append(part)
        for pol in range(2 * pols):
            tile = slice(pol // PACK * LANES, (pol // PACK + 1) * LANES)
            packed = jnp.zeros((2 * SG, LANES), jnp.float32)
            for k in range(PACK):
                move = (k - pol) % PACK * SG
                part = parts[k][:, tile]
                part = pltpu.roll(part, move, 1) if move else part
                packed = jnp.where(slot == k, part, packed)
            out_ref = own_ref if pol < pols else other_ref
            out_ref[pol % pols, group] = packed.astype(jnp.bfloat16)

    for group in range(SETS):
        finish(group)


def grid_rows(place, taps, rows, row_len, half, after, begun=None, ends=True):
    lines = rows[0].shape[1]
    sources = len(rows) * rows[0].shape[0]
    pols = lines // 4
    sums = (NSUB, 2 * SG, 4 * pols * SG)
    done = jax.ShapeDtypeStruct((pols, SETS, 2 * SG, LANES), jnp.bfloat16)
    done = [done] * 2 if ends else [jax.ShapeDtypeStruct(sums, jnp.float32)]
    begun = [] if begun is None else [begun]
    vmem = pl.BlockSpec(memory_space=pltpu.VMEM)
    flops = 2 * sources * row_len * 2 * SG * 4 * pols * SG
    return pl.pallas_call(
        functools.partial(
            grid_kernel,
            row_len=row_len,
            half=half,
            parts=len(rows),
            begins=not begun,
            ends=ends,
        ),
        out_shape=done,
        grid_spec=pltpu.PrefetchScalarGridSpec(
            num_scalar_prefetch=1,
            grid=(),
            in_specs=[vmem] * (1 + len(rows) + len(begun))
            + [pl.BlockSpec(memory_space=pl.ANY)] * len(after),
            out_specs=[vmem] * len(done),
            scratch_shapes=[
                pltpu.VMEM(sums, jnp.float32),
                pltpu.VMEM((sources, LANES), jnp.int32),
                pltpu.SMEM((sources, LANES), jnp.int32),
                pltpu.SemaphoreType.DMA(()),
            ],
        ),
        compiler_params=pltpu.CompilerParams(vmem_limit_bytes=16 << 20),
        cost_estimate=pl.CostEstimate(
            flops=flops * 8, bytes_accessed=2 << 20, transcendentals=0
        ),
        name="grid_rows",
    )(place, taps, *rows, *begun, *after)


def add_kernel(*refs, terms):
    total = refs[0][...].astype(jnp.float32)
    for ref in refs[1:terms]:
        total = total + ref[...].astype(jnp.float32)
    refs[-1][...] = total.astype(jnp.bfloat16)


def add(terms, after=()):
    vmem = pl.BlockSpec(memory_space=pltpu.VMEM)
    return pl.pallas_call(
        functools.partial(add_kernel, terms=len(terms)),
        out_shape=jax.ShapeDtypeStruct(terms[0].shape, jnp.bfloat16),
        in_specs=[vmem] * len(terms) + [pl.BlockSpec(memory_space=pl.ANY)] * len(after),
        out_specs=vmem,
        compiler_params=pltpu.CompilerParams(vmem_limit_bytes=4 << 20),
        cost_estimate=pl.CostEstimate(flops=1 << 18, bytes_accessed=4 << 20, transcendentals=0),
        name="add_sums",
    )(*terms, *after)


def wrapped(value, period):
    if period & (period - 1):
        return jnp.mod(value, period)
    return value & (period - 1)


def circle(phase, period):
    phase = wrapped(phase, period)
    quarter = lax.div(phase + period // 8, period // 4)
    rest = phase - quarter * (period // 4)
    angle = rest.astype(jnp.float32) * (2.0 * math.pi / period)
    square = angle * angle
    sin = -1.0 / 5040 + square * (1.0 / 362880)
    sin = -1.0 / 6 + square * (1.0 / 120 + square * sin)
    sin = angle + angle * square * sin
    cos = -1.0 / 720 + square * (1.0 / 40320)
    cos = 1.0 + square * (-0.5 + square * (1.0 / 24 + square * cos))
    odd = (quarter & 1) == 1
    full_cos, full_sin = jnp.where(odd, sin, cos), jnp.where(odd, cos, sin)
    full_cos = jnp.where(((quarter + 1) & 2) == 2, -full_cos, full_cos)
    return full_cos, jnp.where((quarter & 2) == 2, -full_sin, full_sin)


def tables_kernel(facet_ref, listed_ref, count_ref, *refs, period):
    table_ref, turn_ref, keep_ref = refs[-3:]
    facet = facet_ref[0]
    span = period // SG
    cells = PACK * SG
    row = lax.broadcasted_iota(jnp.int32, (cells, LANES), 0)
    lane = lax.broadcasted_iota(jnp.int32, (cells, LANES), 1)
    tiles = table_ref.shape[1] // LANES
    room = LANES // PACK
    turn_shape = (FY, 2 * PACK * SG)
    turn_line = lax.broadcasted_iota(jnp.int32, turn_shape, 0) - FY // 2
    turn_lane = lax.broadcasted_iota(jnp.int32, turn_shape, 1)
    second = (turn_lane >> 5 & 1) == 1

    def col_cell(group):
        sub = group * PACK + (row >> 5)
        return (wrapped(sub * 53 + 5, span) - span // 2) * SG + (row & (SG - 1))

    tile_id = lane & (room - 1)
    start = jnp.where(tile_id == tiles - 1, -MARGIN, tile_id * LANES)
    start = facet * FX - period // 2 + start
    for batch in range(SETS // PACK):
        coarse_cos, coarse_sin = circle(col_cell(batch * PACK + (lane >> 5)) * start, period)
        for k in range(PACK):
            group = batch * PACK + k
            base = group * 2 * cells
            fine_cos, fine_sin = circle(col_cell(group) * lane, period)
            for tile in range(tiles):
                columns = slice(tile * LANES, (tile + 1) * LANES)
                at = k * room + tile
                tile_cos = coarse_cos[:, at : at + 1]
                tile_neg = -coarse_sin[:, at : at + 1]
                full_cos = tile_cos * fine_cos + tile_neg * fine_sin
                full_neg = tile_neg * fine_cos - tile_cos * fine_sin
                table_ref[base : base + cells, columns] = full_cos.astype(jnp.bfloat16)
                table_ref[base + cells : base + 2 * cells, columns] = full_neg.astype(
                    jnp.bfloat16
                )

            sub = group * PACK + (turn_lane >> 6)
            cell = (wrapped(sub * 37, span) - span // 2) * SG + (turn_lane & (SG - 1))
            cos, sin = circle(cell * turn_line, period)
            turn_ref[group, :FY] = jnp.where(second, -sin, cos).astype(jnp.bfloat16)
            turn_ref[group, FY:] = jnp.where(second, cos, sin).astype(jnp.bfloat16)

    line = lax.broadcasted_iota(jnp.int32, (FY, MARGIN), 0)
    before = jnp.maximum(facet - 1, 0)
    in_use = jnp.where(facet > 0, count_ref[before], 0)

    def mark(k, keep):
        return jnp.where((line == listed_ref[before, k]) & (k < in_use), 1.0, keep)

    keep_ref[...] = lax.fori_loop(
        0, listed_ref.shape[1], mark, jnp.zeros((FY, MARGIN), jnp.float32)
    )


def make_tables(facet, listed, counts, period, token):
    depth, width = 2 * NSUB * SG, FX + MARGIN
    vmem = pl.BlockSpec(memory_space=pltpu.VMEM)
    return pl.pallas_call(
        functools.partial(tables_kernel, period=period),
        out_shape=[
            jax.ShapeDtypeStruct((depth, width), jnp.bfloat16),
            jax.ShapeDtypeStruct((SETS, 2 * FY, 2 * PACK * SG), jnp.bfloat16),
            jax.ShapeDtypeStruct((FY, MARGIN), jnp.float32),
        ],
        grid_spec=pltpu.PrefetchScalarGridSpec(
            num_scalar_prefetch=3,
            grid=(),
            in_specs=[pl.BlockSpec(memory_space=pl.ANY)],
            out_specs=[vmem] * 3,
        ),
        compiler_params=pltpu.CompilerParams(vmem_limit_bytes=16 << 20),
        cost_estimate=pl.CostEstimate(
            flops=8 * depth * width, bytes_accessed=2 * depth * width, transcendentals=1 << 19
        ),
        name="make_tables",
    )(facet, listed, counts, token)


def image_kernel(z1_ref, z0_ref, x_ref, *refs, places, scale, columns):
    parts = len(places)
    piece_refs = refs[:parts]
    turn_ref, table_ref, keep_ref = refs[parts : parts + 3]
    out_ref, lines_ref, done_ref, sems = refs[-4:]
    per = piece_refs[0].shape[0]
    width = table_ref.shape[1] - MARGIN
    slot = lax.broadcasted_iota(jnp.int32, (2 * SG, 2 * LANES), 1) % LANES // SG
    flat = [(part, i) for part in range(parts) for i in range(per)]

    def group_rows(group):
        base = group * 2 * LANES
        for k in range(0, len(flat), 2):
            pair = [piece_refs[part][i, group] for part, i in flat[k : k + 2]]
            pair = jnp.concatenate(pair, axis=1)
            zero = jnp.zeros_like(pair)
            spread = [jnp.where(slot[:, : pair.shape[1]] == s, pair, zero) for s in range(PACK)]
            spread = jnp.concatenate(spread, axis=0)
            turned = jnp.dot(turn_ref[group], spread, preferred_element_type=jnp.float32)
            turned = (turned * scale).astype(jnp.bfloat16)
            for m in range(pair.shape[1] // LANES):
                for q in range(2):
                    lines_ref[
                        (k + m) * FY : (k + m + 1) * FY, base + q * LANES : base + (q + 1) * LANES
                    ] = turned[q * FY : (q + 1) * FY, m * LANES : (m + 1) * LANES]

    for group in range(SETS):
        group_rows(group)
    lines = lines_ref[...]

    def spot(part):
        z_step, x_step, east, half = places[part]
        share = lax.rem(z0_ref[0] + z1_ref[0] + z_step, 2) * east
        share = share + lax.rem(x_ref[0] + east - x_step, east)
        return (share * 2 + half) * per

    def copy(step, part):
        return pltpu.make_async_copy(
            done_ref.at[step % 2, pl.ds(part * per, per)],
            out_ref.at[pl.ds(spot(part), per), :, pl.ds(step * columns, columns)],
            sems.at[step % 2, part],
        )

    steps = width // columns
    for step in range(steps):
        if step >= 2:
            for part in range(parts):
                copy(step - 2, part).wait()
        block = table_ref[:, step * columns : (step + 1) * columns]
        total = jnp.dot(lines, block, preferred_element_type=jnp.float32)
        done_ref[step % 2] = total.reshape(parts * per, FY, columns)
        if step == 0:
            edge = jnp.dot(lines, table_ref[:, width:], preferred_element_type=jnp.float32)
            edge = edge.reshape(parts * per, FY, MARGIN) * keep_ref[...][None]
            done_ref[0, :, :, :MARGIN] += edge
        for part in range(parts):
            copy(step, part).start()
    for step in range(max(steps - 2, 0), steps):
        for part in range(parts):
            copy(step, part).wait()


def add_image(image, device, places, pieces, turn, table, keep, total_pols, scale, after):
    parts, per = len(pieces), pieces[0].shape[0]
    pols = parts * per
    columns = 1024
    depth = table.shape[0]
    width = table.shape[1] - MARGIN
    vmem = pl.BlockSpec(memory_space=pltpu.VMEM)
    operands = [*pieces, turn, table, keep]
    in_specs = [vmem] * len(operands)
    operands.extend(after)
    in_specs.extend([pl.BlockSpec(memory_space=pl.ANY)] * len(after))
    aliases = {}
    if image is not None:
        operands.append(image)
        in_specs.append(pl.BlockSpec(memory_space=pl.ANY))
        aliases = {len(operands) + 2: 0}
    return pl.pallas_call(
        functools.partial(image_kernel, places=places, scale=scale, columns=columns),
        out_shape=jax.ShapeDtypeStruct((total_pols, FY, width), jnp.float32),
        grid_spec=pltpu.PrefetchScalarGridSpec(
            num_scalar_prefetch=3,
            grid=(),
            in_specs=in_specs,
            out_specs=pl.BlockSpec(memory_space=pl.ANY),
            scratch_shapes=[
                pltpu.VMEM((pols * FY, depth), jnp.bfloat16),
                pltpu.VMEM((2, pols, FY, columns), jnp.float32),
                pltpu.SemaphoreType.DMA((2, parts)),
            ],
        ),
        input_output_aliases=aliases,
        compiler_params=pltpu.CompilerParams(vmem_limit_bytes=28 << 20),
        cost_estimate=pl.CostEstimate(
            flops=2 * pols * FY * depth * width,
            bytes_accessed=2 * depth * width + 4 * pols * FY * width,
            transcendentals=0,
        ),
        name="add_image",
    )(*device, *operands)


def shards(
    visibilities, w_kernel, w_index, cell_offsets, block_sub, intersection_rows, intersection_count
):
    cores, east = lax.axis_size("core"), lax.axis_size("x")
    north, upper = lax.axis_size("y"), lax.axis_size("z0")
    groups, facets = north * cores, lax.axis_size(FACET)
    num_chans, num_parts, _, row_len = visibilities.shape
    num_pols = num_parts // 2
    own_chans = num_chans // groups
    shares = upper * east
    chan_shares = math.gcd(shares, own_chans)
    pol_shares = shares // chan_shares
    per_chan, per_pol = own_chans // chan_shares, num_pols // pol_shares
    lines = 2 * per_chan * per_pol
    period = FX * facets
    z1, z0, x = (lax.axis_index(axis) for axis in ("z1", "z0", "x"))

    def scalar(value):
        return jnp.reshape(value, (1,)).astype(jnp.int32)

    vis = visibilities.reshape(num_chans, num_parts, row_len)
    inner = ("y", "z0", "x")
    apart = north == upper == east == 2
    sent = pack_rows(
        [scalar(lax.axis_index(CHAN)), scalar(lax.axis_index(inner)), scalar(z1)],
        vis,
        w_index,
        cell_offsets,
        block_sub,
        (chan_shares, pol_shares, per_chan, per_pol, cores, east),
        north * shares,
        lines,
        apart,
    )
    if apart:
        rows = [sent[0]]
        for k in range(1, len(sent)):
            route = [(i, i ^ k) for i in range(len(sent))]
            rows.append(lax.ppermute(sent[k], inner, route))
    else:
        rows = [lax.all_to_all(sent[0], inner, split_axis=0, concat_axis=0, tiled=True)]
    taps = w_kernel.transpose(1, 2, 0).reshape(-1, w_kernel.shape[0])
    place = scalar(lax.axis_index("core"))
    scale = 1.0 / math.sqrt(groups * facets * row_len)

    def gridded(half, after):
        begun, left = None, rows
        if half == 0 and len(rows) > 1:
            left = [rows[k] for k in LATE]
            begun = [rows[k] for k in range(len(rows)) if k not in LATE]
            begun = grid_rows(place, taps, begun, row_len, half, after, ends=False)[0]
        own, other = grid_rows(place, taps, left, row_len, half, after, begun)
        return own, swap(other, "core")

    def shifted(piece, z_step, x_step):
        if z_step + x_step == 0:
            return piece
        route = [
            (a * east + b, (a + z_step) % upper * east + (b + x_step) % east)
            for a in range(upper)
            for b in range(east)
        ]
        return lax.ppermute(piece, ("z0", "x"), route)

    def gathered(mine, relay):
        pieces = []
        for z_step in range(upper):
            here = shifted(mine, z_step, 0)
            for x_step in range(east):
                if relay or z_step + x_step == 0:
                    pieces.append(shifted(here, 0, x_step))
                else:
                    pieces.append(shifted(mine, z_step, x_step))
        return pieces

    def mirrored(block):
        return lax.ppermute(block, ("z1", "z0"), [(i, 3 - i) for i in range(4)])

    first = add(gridded(0, ()))
    first_far = mirrored(first)
    second = gridded(1, (first,))
    first = add((first, first_far), second[:1])
    second = add(second, (first,))
    second_far = mirrored(second)
    first_pieces = gathered(first, False)
    table, turn, keep = make_tables(
        scalar(lax.axis_index(FACET)), intersection_rows, intersection_count, period, first
    )
    second = add((second, second_far))
    second_pieces = gathered(second, False)
    total_pols = own_chans * num_pols
    device = [scalar(lax.axis_index(axis)) for axis in ("z1", "z0", "x")]
    places = [
        [(a, b, east, half) for a in range(upper) for b in range(east)] for half in range(2)
    ]
    pieces = first_pieces + second_pieces
    places = places[0] + places[1]
    parts = len(first_pieces)
    image = None
    calls = (
        [*range(east), parts],
        range(east, parts),
        range(parts + 1, 2 * parts - 1),
        [2 * parts - 1],
    )
    for chosen in calls:
        image = add_image(
            image,
            device,
            [places[k] for k in chosen],
            [pieces[k] for k in chosen],
            turn,
            table,
            keep,
            total_pols,
            scale,
            (second,),
        )
    return image.reshape(own_chans, num_pols, FY, FX)


def solution(mesh):
    groups, facets = mesh.shape["chan"], mesh.shape["facet"]
    inner = Mesh(
        mesh.devices.reshape(groups // 2, 2, 2, 2, facets // 4), CHAN + FACET
    )
    return jax.shard_map(
        shards,
        mesh=inner,
        in_specs=(
            P(None, None, CHAN, FACET),
            P(),
            P(None, FACET),
            P(None, None, FACET),
            P(None, FACET),
            P(),
            P(),
        ),
        out_specs=P(CHAN, None, None, FACET),
        check_vma=False,
    )
```

```python
import functools
import math

import jax
import jax.numpy as jnp
from jax import lax
from jax.experimental import pallas as pl
from jax.experimental.pallas import tpu as pltpu
from jax.sharding import Mesh
from jax.sharding import PartitionSpec as P

BLK = 512
SG = 32
NSUB = 32
FX = 2048
FY = 64
MARGIN = 128
LANES = 128
PACK = LANES // SG
SETS = NSUB // PACK
CHAN = ("y", "core")
VMEM_LIMIT = 56 << 20
FACET = ("z1", "z0", "x")


def swap(block, axis):
    return lax.ppermute(block, axis, [(0, 1), (1, 0)])


def pack_kernel(
    group_ref, first_ref, flip_ref, vis_from, plane_from, cell_from, sub_from, *refs, shares
):
    out_refs = refs[:-6]
    vis_ref, plane_ref, cell_ref, sub_ref, sems, vis_sem = refs[-6:]
    chan_shares, pol_shares, per_chan, per_pol, cores, east = shares
    all_shares = chan_shares * pol_shares
    num_pols = vis_ref.shape[1] // 2
    row_len = vis_ref.shape[2]
    dests, lines = out_refs[0].shape[0] * len(out_refs), out_refs[0].shape[1]
    width = row_len // lines
    half = per_pol // 2
    group = group_ref[0]
    small = [(plane_from, plane_ref), (cell_from, cell_ref), (sub_from, sub_ref)]
    small = [pltpu.make_async_copy(*pair, sems.at[k]) for k, pair in enumerate(small)]
    large = pltpu.make_async_copy(vis_from, vis_ref, vis_sem)
    for copy in [large] + small:
        copy.start()
    for copy in small:
        copy.wait()

    def folded(row):
        row = row.astype(jnp.float32)
        return jnp.concatenate([row[:, k * width : (k + 1) * width] for k in range(lines)], axis=0)

    def listed(group):
        subs = sub_ref[pl.ds(group, 1), :].astype(jnp.float32)
        subs = jnp.concatenate([subs, jnp.zeros((1, LANES - subs.shape[1]), jnp.float32)], axis=1)
        found = [
            folded(plane_ref[pl.ds(group, 1), :]),
            folded(cell_ref[0, pl.ds(group, 1), :]),
            folded(cell_ref[1, pl.ds(group, 1), :]),
            jnp.broadcast_to(subs, (lines, LANES)),
        ]
        return jnp.concatenate(found, axis=1).astype(jnp.bfloat16)

    ids = listed(group)
    if len(out_refs) > 1:
        ids = jnp.concatenate([ids, listed(group ^ cores)], axis=1)
    large.wait()
    for k in range(dests):
        dest = first_ref[0] ^ k if len(out_refs) > 1 else k
        north, share = lax.div(dest, all_shares), lax.rem(dest, all_shares)
        share = lax.rem(lax.div(share, east) + flip_ref[0], 2) * east + lax.rem(share, east)
        chan_share, pol_share = lax.div(share, pol_shares), lax.rem(share, pol_shares)
        found = ([], [])
        for core in range(cores):
            chan = ((north * cores + core) * chan_shares + chan_share) * per_chan
            chans = [vis_ref[chan + i].astype(jnp.float32) for i in range(per_chan)]
            for part in range(2):
                for vis in chans:
                    rows = vis[part * num_pols : part * num_pols + per_pol]
                    for other in range(1, pol_shares):
                        start = part * num_pols + other * per_pol
                        rows = jnp.where(pol_share == other, vis[start : start + per_pol], rows)
                    found[0].append(rows[:half])
                    found[1].append(rows[half:])
        ref, slot = (out_refs[k], 0) if len(out_refs) > 1 else (out_refs[0], k)
        ref[slot, :, :row_len] = jnp.concatenate(found[0], 0).astype(jnp.bfloat16)
        ref[slot, :, row_len : 2 * row_len] = jnp.concatenate(found[1], 0).astype(jnp.bfloat16)
        if ref.shape[2] > 2 * row_len:
            ref[slot, :, 2 * row_len :] = ids


def pack_rows(device, vis, planes, cells, subs, shares, dests, lines, apart):
    row_len = vis.shape[2]
    ids = 3 * row_len // lines + LANES
    widths = [2 * row_len + ids]
    if apart:
        widths = [2 * row_len + 2 * ids] * (dests // 2) + [2 * row_len] * (dests // 2)
    count = len(widths)
    vmem = pl.BlockSpec(memory_space=pltpu.VMEM)
    return pl.pallas_call(
        functools.partial(pack_kernel, shares=shares),
        out_shape=[
            jax.ShapeDtypeStruct((dests // count, lines, width), jnp.bfloat16) for width in widths
        ],
        grid_spec=pltpu.PrefetchScalarGridSpec(
            num_scalar_prefetch=3,
            grid=(),
            in_specs=[pl.BlockSpec(memory_space=pl.ANY)] * 4,
            out_specs=[vmem] * count,
            scratch_shapes=[pltpu.VMEM(a.shape, a.dtype) for a in (vis, planes, cells, subs)]
            + [pltpu.SemaphoreType.DMA((3,)), pltpu.SemaphoreType.DMA(())],
        ),
        compiler_params=pltpu.CompilerParams(vmem_limit_bytes=VMEM_LIMIT),
        cost_estimate=pl.CostEstimate(flops=1 << 20, bytes_accessed=3 << 20, transcendentals=0),
        name="pack_rows",
    )(*device, vis, planes, cells, subs)


def grid_kernel(place_ref, taps_ref, *refs, row_len, half, slots, begins, ends):
    parts = len(slots)
    rows_refs, ids_refs = refs[:parts], refs[parts : 2 * parts]
    sums_ref, listed_ref, sub_ref, sem = refs[-4:]
    each, lines = rows_refs[0].shape[:2]
    sources = parts * each
    pols = lines // 4
    cells = 2 * pols * SG
    blocks = row_len // BLK
    width = row_len // lines

    ids_width = 3 * width + LANES
    ids_from = [2 * row_len + slot * ids_width for slot in slots]
    for source in range(sources):
        part = source // each
        start = ids_from[part] + 3 * width
        subs = ids_refs[part][source % each, :, start : start + LANES]
        subs = subs.astype(jnp.float32)
        listed_ref[source : source + 1] = subs[:1].astype(jnp.int32)
    copy = pltpu.make_async_copy(listed_ref, sub_ref, sem)
    copy.start()
    sums_ref[...] = jnp.zeros_like(sums_ref) if begins else refs[2 * parts][...]
    copy.wait()
    taps = taps_ref[...].astype(jnp.float32)
    taps = jnp.concatenate([taps, jnp.zeros((16, LANES - taps.shape[1]), jnp.float32)], axis=1)
    cell = lax.broadcasted_iota(jnp.int32, (8, BLK), 0)

    def listed(ids, kind, block):
        found = []
        for start in range(block * BLK, (block + 1) * BLK, min(BLK, width)):
            line, column = start // width, kind * width + start % width
            found.append(ids[line : line + 1, column : column + min(BLK, width)])
        return jnp.concatenate(found, axis=1) if len(found) > 1 else found[0]

    def pick(values, index, axis):
        found = [
            jnp.take_along_axis(
                values if axis else values[:, c : c + LANES], index[:, c : c + LANES], axis=axis
            )
            for c in range(0, BLK, LANES)
        ]
        return jnp.concatenate(found, axis=1)

    level = -(lax.broadcasted_iota(jnp.int32, (16, BLK), 0) >> 3)
    levels = [(level - 2 * k).astype(jnp.float32).astype(jnp.bfloat16) for k in range(SG // 16)]
    none = jnp.zeros((16, BLK), jnp.bfloat16)

    def doubled(part):
        return jnp.concatenate([part, part], axis=0).astype(jnp.bfloat16)

    def turned(values, offset):
        distance = cell - offset
        height = doubled((distance >> 3).astype(jnp.float32))
        parts = [pick(values[8 * q : 8 * q + 8], distance & 7, 0) for q in range(2)]
        return parts, [height == level for level in levels]

    def spread(part, masks):
        part = doubled(part)
        return jnp.concatenate([jnp.where(mask, part, none) for mask in masks], axis=0)

    def grid_source(part, slot, source):
        rows_ref = rows_refs[part]
        ids = ids_refs[part][slot, :, ids_from[part] : ids_from[part] + 3 * width]
        ids = ids.astype(jnp.float32).astype(jnp.int32)
        for block in range(blocks):
            plane = jnp.broadcast_to(listed(ids, 0, block), (16, BLK))
            values = pick(taps, plane, 1)
            parts, masks = turned(values, listed(ids, 1, block))
            left = jnp.concatenate([spread(part, masks) for part in parts], axis=0)
            (kern_re, kern_im), masks = turned(values, listed(ids, 2, block))
            start = half * row_len + block * BLK
            vis = rows_ref[slot, :, start : start + BLK].astype(jnp.float32)
            vis = pltpu.roll(vis, place_ref[0] * (lines // 2), 0)
            real, imag = [], []
            for first in (0, 2 * pols):
                for row in range(first, first + pols):
                    vis_re = vis[row : row + 1]
                    vis_im = vis[row + pols : row + pols + 1]
                    real.append(spread(vis_re * kern_re - vis_im * kern_im, masks))
                    imag.append(spread(vis_re * kern_im + vis_im * kern_re, masks))
            weighted = jnp.concatenate(real + imag, axis=0)
            sub = sub_ref[source, block]
            sums_ref[sub] += lax.dot_general(
                left, weighted, (((1,), (1,)), ((), ())), preferred_element_type=jnp.float32
            )

    unroll = math.gcd(each, 4)

    def grid_sources(step, carry):
        for k in range(unroll):
            slot = step * unroll + k
            grid_source(0, slot, slot)
        return carry

    if parts > 1:
        for source in range(sources):
            grid_source(source // each, source % each, source)
    else:
        lax.fori_loop(0, each // unroll, grid_sources, 0)
    if not ends:
        refs[-5][...] = sums_ref[...]
        return
    own_ref, other_ref = refs[-6:-4]
    slot = lax.broadcasted_iota(jnp.int32, (2 * SG, LANES), 1) // SG

    def finish(group):
        parts = []
        for k in range(PACK):
            raw = sums_ref[group * PACK + k]
            real = raw[:SG, :cells] - raw[SG:, cells:]
            imag = raw[:SG, cells:] + raw[SG:, :cells]
            part = jnp.concatenate([real, imag], axis=0)
            if cells < LANES:
                part = jnp.concatenate([part, jnp.zeros_like(part)], axis=1)
            parts.append(part)
        for pol in range(2 * pols):
            tile = slice(pol // PACK * LANES, (pol // PACK + 1) * LANES)
            packed = jnp.zeros((2 * SG, LANES), jnp.float32)
            for k in range(PACK):
                move = (k - pol) % PACK * SG
                part = parts[k][:, tile]
                part = pltpu.roll(part, move, 1) if move else part
                packed = jnp.where(slot == k, part, packed)
            out_ref = own_ref if pol < pols else other_ref
            out_ref[pol % pols, group] = packed.astype(jnp.bfloat16)

    for group in range(SETS):
        finish(group)


def grid_rows(place, taps, rows, ids, slots, row_len, half, after, begun=None, ends=True):
    lines = rows[0].shape[1]
    sources = len(rows) * rows[0].shape[0]
    pols = lines // 4
    sums = (NSUB, 2 * SG, 4 * pols * SG)
    done = jax.ShapeDtypeStruct((pols, SETS, 2 * SG, LANES), jnp.bfloat16)
    done = [done] * 2 if ends else [jax.ShapeDtypeStruct(sums, jnp.float32)]
    begun = [] if begun is None else [begun]
    vmem = pl.BlockSpec(memory_space=pltpu.VMEM)
    flops = 2 * sources * row_len * 2 * SG * 4 * pols * SG
    return pl.pallas_call(
        functools.partial(
            grid_kernel,
            row_len=row_len,
            half=half,
            slots=slots,
            begins=not begun,
            ends=ends,
        ),
        out_shape=done,
        grid_spec=pltpu.PrefetchScalarGridSpec(
            num_scalar_prefetch=1,
            grid=(),
            in_specs=[vmem] * (1 + 2 * len(rows) + len(begun))
            + [pl.BlockSpec(memory_space=pl.ANY)] * len(after),
            out_specs=[vmem] * len(done),
            scratch_shapes=[
                pltpu.VMEM(sums, jnp.float32),
                pltpu.VMEM((sources, LANES), jnp.int32),
                pltpu.SMEM((sources, LANES), jnp.int32),
                pltpu.SemaphoreType.DMA(()),
            ],
        ),
        compiler_params=pltpu.CompilerParams(vmem_limit_bytes=16 << 20),
        cost_estimate=pl.CostEstimate(
            flops=flops * 8, bytes_accessed=2 << 20, transcendentals=0
        ),
        name="grid_rows",
    )(place, taps, *rows, *ids, *begun, *after)


def add_kernel(*refs, terms):
    total = refs[0][...].astype(jnp.float32)
    for ref in refs[1:terms]:
        total = total + ref[...].astype(jnp.float32)
    refs[-1][...] = total.astype(jnp.bfloat16)


def add(terms, after=()):
    vmem = pl.BlockSpec(memory_space=pltpu.VMEM)
    return pl.pallas_call(
        functools.partial(add_kernel, terms=len(terms)),
        out_shape=jax.ShapeDtypeStruct(terms[0].shape, jnp.bfloat16),
        in_specs=[vmem] * len(terms) + [pl.BlockSpec(memory_space=pl.ANY)] * len(after),
        out_specs=vmem,
        compiler_params=pltpu.CompilerParams(vmem_limit_bytes=4 << 20),
        cost_estimate=pl.CostEstimate(flops=1 << 18, bytes_accessed=4 << 20, transcendentals=0),
        name="add_sums",
    )(*terms, *after)


def wrapped(value, period):
    if period & (period - 1):
        return jnp.mod(value, period)
    return value & (period - 1)


def circle(phase, period):
    phase = wrapped(phase, period)
    quarter = lax.div(phase + period // 8, period // 4)
    rest = phase - quarter * (period // 4)
    angle = rest.astype(jnp.float32) * (2.0 * math.pi / period)
    square = angle * angle
    sin = -1.0 / 5040 + square * (1.0 / 362880)
    sin = -1.0 / 6 + square * (1.0 / 120 + square * sin)
    sin = angle + angle * square * sin
    cos = -1.0 / 720 + square * (1.0 / 40320)
    cos = 1.0 + square * (-0.5 + square * (1.0 / 24 + square * cos))
    odd = (quarter & 1) == 1
    full_cos, full_sin = jnp.where(odd, sin, cos), jnp.where(odd, cos, sin)
    full_cos = jnp.where(((quarter + 1) & 2) == 2, -full_cos, full_cos)
    return full_cos, jnp.where((quarter & 2) == 2, -full_sin, full_sin)


def tables_kernel(facet_ref, listed_ref, count_ref, *refs, period):
    table_ref, turn_ref, keep_ref = refs[-3:]
    facet = facet_ref[0]
    span = period // SG
    cells = PACK * SG
    row = lax.broadcasted_iota(jnp.int32, (cells, LANES), 0)
    lane = lax.broadcasted_iota(jnp.int32, (cells, LANES), 1)
    tiles = table_ref.shape[1] // LANES
    room = LANES // PACK
    turn_shape = (FY, 2 * PACK * SG)
    turn_line = lax.broadcasted_iota(jnp.int32, turn_shape, 0) - FY // 2
    turn_lane = lax.broadcasted_iota(jnp.int32, turn_shape, 1)
    second = (turn_lane >> 5 & 1) == 1

    def col_cell(group):
        sub = group * PACK + (row >> 5)
        return (wrapped(sub * 53 + 5, span) - span // 2) * SG + (row & (SG - 1))

    tile_id = lane & (room - 1)
    start = jnp.where(tile_id == tiles - 1, -MARGIN, tile_id * LANES)
    start = facet * FX - period // 2 + start
    for batch in range(SETS // PACK):
        coarse_cos, coarse_sin = circle(col_cell(batch * PACK + (lane >> 5)) * start, period)
        for k in range(PACK):
            group = batch * PACK + k
            base = group * 2 * cells
            fine_cos, fine_sin = circle(col_cell(group) * lane, period)
            for tile in range(tiles):
                columns = slice(tile * LANES, (tile + 1) * LANES)
                at = k * room + tile
                tile_cos = coarse_cos[:, at : at + 1]
                tile_neg = -coarse_sin[:, at : at + 1]
                full_cos = tile_cos * fine_cos + tile_neg * fine_sin
                full_neg = tile_neg * fine_cos - tile_cos * fine_sin
                table_ref[base : base + cells, columns] = full_cos.astype(jnp.bfloat16)
                table_ref[base + cells : base + 2 * cells, columns] = full_neg.astype(
                    jnp.bfloat16
                )

            sub = group * PACK + (turn_lane >> 6)
            cell = (wrapped(sub * 37, span) - span // 2) * SG + (turn_lane & (SG - 1))
            cos, sin = circle(cell * turn_line, period)
            turn_ref[group, :FY] = jnp.where(second, -sin, cos).astype(jnp.bfloat16)
            turn_ref[group, FY:] = jnp.where(second, cos, sin).astype(jnp.bfloat16)

    line = lax.broadcasted_iota(jnp.int32, (FY, MARGIN), 0)
    before = jnp.maximum(facet - 1, 0)
    in_use = jnp.where(facet > 0, count_ref[before], 0)

    def mark(k, keep):
        return jnp.where((line == listed_ref[before, k]) & (k < in_use), 1.0, keep)

    keep_ref[...] = lax.fori_loop(
        0, listed_ref.shape[1], mark, jnp.zeros((FY, MARGIN), jnp.float32)
    )


def make_tables(facet, listed, counts, period, token):
    depth, width = 2 * NSUB * SG, FX + MARGIN
    vmem = pl.BlockSpec(memory_space=pltpu.VMEM)
    return pl.pallas_call(
        functools.partial(tables_kernel, period=period),
        out_shape=[
            jax.ShapeDtypeStruct((depth, width), jnp.bfloat16),
            jax.ShapeDtypeStruct((SETS, 2 * FY, 2 * PACK * SG), jnp.bfloat16),
            jax.ShapeDtypeStruct((FY, MARGIN), jnp.float32),
        ],
        grid_spec=pltpu.PrefetchScalarGridSpec(
            num_scalar_prefetch=3,
            grid=(),
            in_specs=[pl.BlockSpec(memory_space=pl.ANY)],
            out_specs=[vmem] * 3,
        ),
        compiler_params=pltpu.CompilerParams(vmem_limit_bytes=16 << 20),
        cost_estimate=pl.CostEstimate(
            flops=8 * depth * width, bytes_accessed=2 * depth * width, transcendentals=1 << 19
        ),
        name="make_tables",
    )(facet, listed, counts, token)


def image_kernel(z1_ref, z0_ref, x_ref, *refs, places, scale, columns):
    parts = len(places)
    piece_refs = refs[:parts]
    turn_ref, table_ref, keep_ref = refs[parts : parts + 3]
    out_ref, lines_ref, done_ref, sems = refs[-4:]
    per = piece_refs[0].shape[0]
    width = table_ref.shape[1] - MARGIN
    slot = lax.broadcasted_iota(jnp.int32, (2 * SG, 2 * LANES), 1) % LANES // SG
    flat = [(part, i) for part in range(parts) for i in range(per)]

    def group_rows(group):
        base = group * 2 * LANES
        for k in range(0, len(flat), 2):
            pair = [piece_refs[part][i, group] for part, i in flat[k : k + 2]]
            pair = jnp.concatenate(pair, axis=1)
            zero = jnp.zeros_like(pair)
            spread = [jnp.where(slot[:, : pair.shape[1]] == s, pair, zero) for s in range(PACK)]
            spread = jnp.concatenate(spread, axis=0)
            turned = jnp.dot(turn_ref[group], spread, preferred_element_type=jnp.float32)
            turned = (turned * scale).astype(jnp.bfloat16)
            for m in range(pair.shape[1] // LANES):
                for q in range(2):
                    lines_ref[
                        (k + m) * FY : (k + m + 1) * FY, base + q * LANES : base + (q + 1) * LANES
                    ] = turned[q * FY : (q + 1) * FY, m * LANES : (m + 1) * LANES]

    for group in range(SETS):
        group_rows(group)
    lines = lines_ref[...]

    def spot(part):
        z_step, x_step, east, half = places[part]
        share = lax.rem(z0_ref[0] + z1_ref[0] + z_step, 2) * east
        share = share + lax.rem(x_ref[0] + east - x_step, east)
        return (share * 2 + half) * per

    def copy(step, part):
        return pltpu.make_async_copy(
            done_ref.at[step % 2, pl.ds(part * per, per)],
            out_ref.at[pl.ds(spot(part), per), :, pl.ds(step * columns, columns)],
            sems.at[step % 2, part],
        )

    steps = width // columns
    for step in range(steps):
        if step >= 2:
            for part in range(parts):
                copy(step - 2, part).wait()
        block = table_ref[:, step * columns : (step + 1) * columns]
        total = jnp.dot(lines, block, preferred_element_type=jnp.float32)
        done_ref[step % 2] = total.reshape(parts * per, FY, columns)
        if step == 0:
            edge = jnp.dot(lines, table_ref[:, width:], preferred_element_type=jnp.float32)
            edge = edge.reshape(parts * per, FY, MARGIN) * keep_ref[...][None]
            done_ref[0, :, :, :MARGIN] += edge
        for part in range(parts):
            copy(step, part).start()
    for step in range(max(steps - 2, 0), steps):
        for part in range(parts):
            copy(step, part).wait()


def add_image(image, device, places, pieces, turn, table, keep, total_pols, scale, after):
    parts, per = len(pieces), pieces[0].shape[0]
    pols = parts * per
    columns = 1024
    depth = table.shape[0]
    width = table.shape[1] - MARGIN
    vmem = pl.BlockSpec(memory_space=pltpu.VMEM)
    operands = [*pieces, turn, table, keep]
    in_specs = [vmem] * len(operands)
    operands.extend(after)
    in_specs.extend([pl.BlockSpec(memory_space=pl.ANY)] * len(after))
    aliases = {}
    if image is not None:
        operands.append(image)
        in_specs.append(pl.BlockSpec(memory_space=pl.ANY))
        aliases = {len(operands) + 2: 0}
    return pl.pallas_call(
        functools.partial(image_kernel, places=places, scale=scale, columns=columns),
        out_shape=jax.ShapeDtypeStruct((total_pols, FY, width), jnp.float32),
        grid_spec=pltpu.PrefetchScalarGridSpec(
            num_scalar_prefetch=3,
            grid=(),
            in_specs=in_specs,
            out_specs=pl.BlockSpec(memory_space=pl.ANY),
            scratch_shapes=[
                pltpu.VMEM((pols * FY, depth), jnp.bfloat16),
                pltpu.VMEM((2, pols, FY, columns), jnp.float32),
                pltpu.SemaphoreType.DMA((2, parts)),
            ],
        ),
        input_output_aliases=aliases,
        compiler_params=pltpu.CompilerParams(vmem_limit_bytes=28 << 20),
        cost_estimate=pl.CostEstimate(
            flops=2 * pols * FY * depth * width,
            bytes_accessed=2 * depth * width + 4 * pols * FY * width,
            transcendentals=0,
        ),
        name="add_image",
    )(*device, *operands)


def shards(
    visibilities, w_kernel, w_index, cell_offsets, block_sub, intersection_rows, intersection_count
):
    cores, east = lax.axis_size("core"), lax.axis_size("x")
    north, upper = lax.axis_size("y"), lax.axis_size("z0")
    groups, facets = north * cores, lax.axis_size(FACET)
    num_chans, num_parts, _, row_len = visibilities.shape
    num_pols = num_parts // 2
    own_chans = num_chans // groups
    shares = upper * east
    chan_shares = math.gcd(shares, own_chans)
    pol_shares = shares // chan_shares
    per_chan, per_pol = own_chans // chan_shares, num_pols // pol_shares
    lines = 2 * per_chan * per_pol
    period = FX * facets
    z1, z0, x = (lax.axis_index(axis) for axis in ("z1", "z0", "x"))

    def scalar(value):
        return jnp.reshape(value, (1,)).astype(jnp.int32)

    vis = visibilities.reshape(num_chans, num_parts, row_len)
    inner = ("y", "z0", "x")
    apart = north == upper == east == 2
    sent = pack_rows(
        [scalar(lax.axis_index(CHAN)), scalar(lax.axis_index(inner)), scalar(z1)],
        vis,
        w_index,
        cell_offsets,
        block_sub,
        (chan_shares, pol_shares, per_chan, per_pol, cores, east),
        north * shares,
        lines,
        apart,
    )
    if apart:
        rows = [sent[0]]
        for k in range(1, len(sent)):
            route = [(i, i ^ k) for i in range(len(sent))]
            rows.append(lax.ppermute(sent[k], inner, route))
    else:
        rows = [lax.all_to_all(sent[0], inner, split_axis=0, concat_axis=0, tiled=True)]
    taps = w_kernel.transpose(1, 2, 0).reshape(-1, w_kernel.shape[0])
    place = scalar(lax.axis_index("core"))
    scale = 1.0 / math.sqrt(groups * facets * row_len)

    def gridded(half, after):
        parts = len(rows)
        ids = [rows[k % (parts // 2)] for k in range(parts)] if parts > 1 else rows
        slots = [k * 2 // parts for k in range(parts)]
        begun, begin = None, 0
        if half == 0 and parts > 1:
            begun, begin = grid_rows(
                place,
                taps,
                rows[: parts // 2],
                ids[: parts // 2],
                slots[: parts // 2],
                row_len,
                half,
                after,
                ends=False,
            )[0], parts // 2
        own, other = grid_rows(
            place, taps, rows[begin:], ids[begin:], slots[begin:], row_len, half, after, begun
        )
        return own, swap(other, "core")

    def shifted(piece, z_step, x_step):
        if z_step + x_step == 0:
            return piece
        route = [
            (a * east + b, (a + z_step) % upper * east + (b + x_step) % east)
            for a in range(upper)
            for b in range(east)
        ]
        return lax.ppermute(piece, ("z0", "x"), route)

    def gathered(mine, relay):
        pieces = []
        for z_step in range(upper):
            here = shifted(mine, z_step, 0)
            for x_step in range(east):
                if relay or z_step + x_step == 0:
                    pieces.append(shifted(here, 0, x_step))
                else:
                    pieces.append(shifted(mine, z_step, x_step))
        return pieces

    def mirrored(block):
        return lax.ppermute(block, ("z1", "z0"), [(i, 3 - i) for i in range(4)])

    first = add(gridded(0, ()))
    first_far = mirrored(first)
    second = gridded(1, (first,))
    first = add((first, first_far), second[:1])
    second = add(second, (first,))
    second_far = mirrored(second)
    first_pieces = gathered(first, False)
    table, turn, keep = make_tables(
        scalar(lax.axis_index(FACET)), intersection_rows, intersection_count, period, first
    )
    second = add((second, second_far))
    second_pieces = gathered(second, False)
    total_pols = own_chans * num_pols
    device = [scalar(lax.axis_index(axis)) for axis in ("z1", "z0", "x")]
    places = [
        [(a, b, east, half) for a in range(upper) for b in range(east)] for half in range(2)
    ]
    pieces = first_pieces + second_pieces
    places = places[0] + places[1]
    parts = len(first_pieces)
    image = None
    calls = (
        [*range(east), parts],
        range(east, parts),
        range(parts + 1, 2 * parts - 1),
        [2 * parts - 1],
    )
    for chosen in calls:
        image = add_image(
            image,
            device,
            [places[k] for k in chosen],
            [pieces[k] for k in chosen],
            turn,
            table,
            keep,
            total_pols,
            scale,
            (second,),
        )
    return image.reshape(own_chans, num_pols, FY, FX)


def solution(mesh):
    groups, facets = mesh.shape["chan"], mesh.shape["facet"]
    inner = Mesh(
        mesh.devices.reshape(groups // 2, 2, 2, 2, facets // 4), CHAN + FACET
    )
    return jax.shard_map(
        shards,
        mesh=inner,
        in_specs=(
            P(None, None, CHAN, FACET),
            P(),
            P(None, FACET),
            P(None, None, FACET),
            P(None, FACET),
            P(),
            P(),
        ),
        out_specs=P(CHAN, None, None, FACET),
        check_vma=False,
    )
```

```python
import functools
import math

import jax
import jax.numpy as jnp
from jax import lax
from jax.experimental import pallas as pl
from jax.experimental.pallas import tpu as pltpu
from jax.sharding import Mesh
from jax.sharding import PartitionSpec as P

BLK = 512
SG = 32
NSUB = 32
FX = 2048
FY = 64
MARGIN = 128
LANES = 128
PACK = LANES // SG
SETS = NSUB // PACK
CHAN = ("y", "core")
VMEM_LIMIT = 56 << 20
FACET = ("z1", "z0", "x")


def swap(block, axis):
    return lax.ppermute(block, axis, [(0, 1), (1, 0)])


def pack_kernel(
    group_ref, first_ref, flip_ref, vis_from, plane_from, cell_from, sub_from, *refs, shares
):
    out_refs = refs[:-6]
    vis_ref, plane_ref, cell_ref, sub_ref, sems, vis_sem = refs[-6:]
    chan_shares, pol_shares, per_chan, per_pol, cores, east = shares
    all_shares = chan_shares * pol_shares
    num_pols = vis_ref.shape[1] // 2
    row_len = vis_ref.shape[2]
    dests, lines = out_refs[0].shape[0] * len(out_refs), out_refs[0].shape[1]
    width = row_len // lines
    half = per_pol // 2
    group = group_ref[0]
    small = [(plane_from, plane_ref), (cell_from, cell_ref), (sub_from, sub_ref)]
    small = [pltpu.make_async_copy(*pair, sems.at[k]) for k, pair in enumerate(small)]
    large = pltpu.make_async_copy(vis_from, vis_ref, vis_sem)
    for copy in [large] + small:
        copy.start()
    for copy in small:
        copy.wait()

    def folded(row):
        row = row.astype(jnp.float32)
        return jnp.concatenate([row[:, k * width : (k + 1) * width] for k in range(lines)], axis=0)

    def listed(group):
        subs = sub_ref[pl.ds(group, 1), :].astype(jnp.float32)
        subs = jnp.concatenate([subs, jnp.zeros((1, LANES - subs.shape[1]), jnp.float32)], axis=1)
        found = [
            folded(plane_ref[pl.ds(group, 1), :]),
            folded(cell_ref[0, pl.ds(group, 1), :]),
            folded(cell_ref[1, pl.ds(group, 1), :]),
            jnp.broadcast_to(subs, (lines, LANES)),
        ]
        return jnp.concatenate(found, axis=1).astype(jnp.bfloat16)

    ids = listed(group)
    if len(out_refs) > 1:
        ids = jnp.concatenate([ids, listed(group ^ cores)], axis=1)
    large.wait()
    for k in range(dests):
        dest = first_ref[0] ^ k if len(out_refs) > 1 else k
        north, share = lax.div(dest, all_shares), lax.rem(dest, all_shares)
        share = lax.rem(lax.div(share, east) + flip_ref[0], 2) * east + lax.rem(share, east)
        chan_share, pol_share = lax.div(share, pol_shares), lax.rem(share, pol_shares)
        found = ([], [])
        for core in range(cores):
            chan = ((north * cores + core) * chan_shares + chan_share) * per_chan
            chans = [vis_ref[chan + i].astype(jnp.float32) for i in range(per_chan)]
            for part in range(2):
                for vis in chans:
                    rows = vis[part * num_pols : part * num_pols + per_pol]
                    for other in range(1, pol_shares):
                        start = part * num_pols + other * per_pol
                        rows = jnp.where(pol_share == other, vis[start : start + per_pol], rows)
                    found[0].append(rows[:half])
                    found[1].append(rows[half:])
        ref, slot = (out_refs[k], 0) if len(out_refs) > 1 else (out_refs[0], k)
        ref[slot, :, :row_len] = jnp.concatenate(found[0], 0).astype(jnp.bfloat16)
        ref[slot, :, row_len : 2 * row_len] = jnp.concatenate(found[1], 0).astype(jnp.bfloat16)
        if ref.shape[2] > 2 * row_len:
            ref[slot, :, 2 * row_len :] = ids


def pack_rows(device, vis, planes, cells, subs, shares, dests, lines, apart):
    row_len = vis.shape[2]
    ids = 3 * row_len // lines + LANES
    widths = [2 * row_len + ids]
    if apart:
        widths = [2 * row_len + 2 * ids] * (dests // 2) + [2 * row_len] * (dests // 2)
    count = len(widths)
    vmem = pl.BlockSpec(memory_space=pltpu.VMEM)
    return pl.pallas_call(
        functools.partial(pack_kernel, shares=shares),
        out_shape=[
            jax.ShapeDtypeStruct((dests // count, lines, width), jnp.bfloat16) for width in widths
        ],
        grid_spec=pltpu.PrefetchScalarGridSpec(
            num_scalar_prefetch=3,
            grid=(),
            in_specs=[pl.BlockSpec(memory_space=pl.ANY)] * 4,
            out_specs=[vmem] * count,
            scratch_shapes=[pltpu.VMEM(a.shape, a.dtype) for a in (vis, planes, cells, subs)]
            + [pltpu.SemaphoreType.DMA((3,)), pltpu.SemaphoreType.DMA(())],
        ),
        compiler_params=pltpu.CompilerParams(vmem_limit_bytes=VMEM_LIMIT),
        cost_estimate=pl.CostEstimate(flops=1 << 20, bytes_accessed=3 << 20, transcendentals=0),
        name="pack_rows",
    )(*device, vis, planes, cells, subs)


def grid_kernel(place_ref, taps_ref, *refs, row_len, half, slots, begins, ends):
    parts = len(slots)
    rows_refs, ids_refs = refs[:parts], refs[parts : 2 * parts]
    sums_ref, listed_ref, sub_ref, sem = refs[-4:]
    each, lines = rows_refs[0].shape[:2]
    sources = parts * each
    pols = lines // 4
    cells = 2 * pols * SG
    blocks = row_len // BLK
    width = row_len // lines

    ids_width = 3 * width + LANES
    ids_from = [2 * row_len + slot * ids_width for slot in slots]
    for source in range(sources):
        part = source // each
        start = ids_from[part] + 3 * width
        subs = ids_refs[part][source % each, :, start : start + LANES]
        subs = subs.astype(jnp.float32)
        listed_ref[source : source + 1] = subs[:1].astype(jnp.int32)
    copy = pltpu.make_async_copy(listed_ref, sub_ref, sem)
    copy.start()
    sums_ref[...] = jnp.zeros_like(sums_ref) if begins else refs[2 * parts][...]
    copy.wait()
    taps = taps_ref[...].astype(jnp.float32)
    taps = jnp.concatenate([taps, jnp.zeros((16, LANES - taps.shape[1]), jnp.float32)], axis=1)
    cell = lax.broadcasted_iota(jnp.int32, (8, BLK), 0)

    def listed(ids, kind, block):
        found = []
        for start in range(block * BLK, (block + 1) * BLK, min(BLK, width)):
            line, column = start // width, kind * width + start % width
            found.append(ids[line : line + 1, column : column + min(BLK, width)])
        return jnp.concatenate(found, axis=1) if len(found) > 1 else found[0]

    def pick(values, index, axis):
        found = [
            jnp.take_along_axis(
                values if axis else values[:, c : c + LANES], index[:, c : c + LANES], axis=axis
            )
            for c in range(0, BLK, LANES)
        ]
        return jnp.concatenate(found, axis=1)

    level = -(lax.broadcasted_iota(jnp.int32, (16, BLK), 0) >> 3)
    levels = [(level - 2 * k).astype(jnp.float32).astype(jnp.bfloat16) for k in range(SG // 16)]
    none = jnp.zeros((16, BLK), jnp.bfloat16)

    def doubled(part):
        return jnp.concatenate([part, part], axis=0).astype(jnp.bfloat16)

    def turned(values, offset):
        distance = cell - offset
        height = doubled((distance >> 3).astype(jnp.float32))
        parts = [pick(values[8 * q : 8 * q + 8], distance & 7, 0) for q in range(2)]
        return parts, [height == level for level in levels]

    def spread(part, masks):
        part = doubled(part)
        return jnp.concatenate([jnp.where(mask, part, none) for mask in masks], axis=0)

    def grid_source(part, slot, source):
        rows_ref = rows_refs[part]
        ids = ids_refs[part][slot, :, ids_from[part] : ids_from[part] + 3 * width]
        ids = ids.astype(jnp.float32).astype(jnp.int32)
        for block in range(blocks):
            plane = jnp.broadcast_to(listed(ids, 0, block), (16, BLK))
            values = pick(taps, plane, 1)
            parts, masks = turned(values, listed(ids, 1, block))
            left = jnp.concatenate([spread(part, masks) for part in parts], axis=0)
            (kern_re, kern_im), masks = turned(values, listed(ids, 2, block))
            start = half * row_len + block * BLK
            vis = rows_ref[slot, :, start : start + BLK].astype(jnp.float32)
            vis = pltpu.roll(vis, place_ref[0] * (lines // 2), 0)
            real, imag = [], []
            for first in (0, 2 * pols):
                for row in range(first, first + pols):
                    vis_re = vis[row : row + 1]
                    vis_im = vis[row + pols : row + pols + 1]
                    real.append(spread(vis_re * kern_re - vis_im * kern_im, masks))
                    imag.append(spread(vis_re * kern_im + vis_im * kern_re, masks))
            weighted = jnp.concatenate(real + imag, axis=0)
            sub = sub_ref[source, block]
            sums_ref[sub] += lax.dot_general(
                left, weighted, (((1,), (1,)), ((), ())), preferred_element_type=jnp.float32
            )

    unroll = math.gcd(each, 4)

    def grid_sources(step, carry):
        for k in range(unroll):
            slot = step * unroll + k
            grid_source(0, slot, slot)
        return carry

    if parts > 1:
        for source in range(sources):
            grid_source(source // each, source % each, source)
    else:
        lax.fori_loop(0, each // unroll, grid_sources, 0)
    if not ends:
        refs[-5][...] = sums_ref[...]
        return
    own_ref, other_ref = refs[-6:-4]
    slot = lax.broadcasted_iota(jnp.int32, (2 * SG, LANES), 1) // SG

    def finish(group):
        parts = []
        for k in range(PACK):
            raw = sums_ref[group * PACK + k]
            real = raw[:SG, :cells] - raw[SG:, cells:]
            imag = raw[:SG, cells:] + raw[SG:, :cells]
            part = jnp.concatenate([real, imag], axis=0)
            if cells < LANES:
                part = jnp.concatenate([part, jnp.zeros_like(part)], axis=1)
            parts.append(part)
        for pol in range(2 * pols):
            tile = slice(pol // PACK * LANES, (pol // PACK + 1) * LANES)
            packed = jnp.zeros((2 * SG, LANES), jnp.float32)
            for k in range(PACK):
                move = (k - pol) % PACK * SG
                part = parts[k][:, tile]
                part = pltpu.roll(part, move, 1) if move else part
                packed = jnp.where(slot == k, part, packed)
            out_ref = own_ref if pol < pols else other_ref
            out_ref[pol % pols, group] = packed.astype(jnp.bfloat16)

    for group in range(SETS):
        finish(group)


def grid_rows(place, taps, rows, ids, slots, row_len, half, after, begun=None, ends=True):
    lines = rows[0].shape[1]
    sources = len(rows) * rows[0].shape[0]
    pols = lines // 4
    sums = (NSUB, 2 * SG, 4 * pols * SG)
    done = jax.ShapeDtypeStruct((pols, SETS, 2 * SG, LANES), jnp.bfloat16)
    done = [done] * 2 if ends else [jax.ShapeDtypeStruct(sums, jnp.float32)]
    begun = [] if begun is None else [begun]
    vmem = pl.BlockSpec(memory_space=pltpu.VMEM)
    flops = 2 * sources * row_len * 2 * SG * 4 * pols * SG
    return pl.pallas_call(
        functools.partial(
            grid_kernel,
            row_len=row_len,
            half=half,
            slots=slots,
            begins=not begun,
            ends=ends,
        ),
        out_shape=done,
        grid_spec=pltpu.PrefetchScalarGridSpec(
            num_scalar_prefetch=1,
            grid=(),
            in_specs=[vmem] * (1 + 2 * len(rows) + len(begun))
            + [pl.BlockSpec(memory_space=pl.ANY)] * len(after),
            out_specs=[vmem] * len(done),
            scratch_shapes=[
                pltpu.VMEM(sums, jnp.float32),
                pltpu.VMEM((sources, LANES), jnp.int32),
                pltpu.SMEM((sources, LANES), jnp.int32),
                pltpu.SemaphoreType.DMA(()),
            ],
        ),
        compiler_params=pltpu.CompilerParams(vmem_limit_bytes=16 << 20),
        cost_estimate=pl.CostEstimate(
            flops=flops * 8, bytes_accessed=2 << 20, transcendentals=0
        ),
        name="grid_rows",
    )(place, taps, *rows, *ids, *begun, *after)


def add_kernel(*refs, terms):
    total = refs[0][...].astype(jnp.float32)
    for ref in refs[1:terms]:
        total = total + ref[...].astype(jnp.float32)
    refs[-1][...] = total.astype(jnp.bfloat16)


def add(terms, after=()):
    vmem = pl.BlockSpec(memory_space=pltpu.VMEM)
    return pl.pallas_call(
        functools.partial(add_kernel, terms=len(terms)),
        out_shape=jax.ShapeDtypeStruct(terms[0].shape, jnp.bfloat16),
        in_specs=[vmem] * len(terms) + [pl.BlockSpec(memory_space=pl.ANY)] * len(after),
        out_specs=vmem,
        compiler_params=pltpu.CompilerParams(vmem_limit_bytes=4 << 20),
        cost_estimate=pl.CostEstimate(flops=1 << 18, bytes_accessed=4 << 20, transcendentals=0),
        name="add_sums",
    )(*terms, *after)


def wrapped(value, period):
    if period & (period - 1):
        return jnp.mod(value, period)
    return value & (period - 1)


def circle(phase, period):
    phase = wrapped(phase, period)
    quarter = lax.div(phase + period // 8, period // 4)
    rest = phase - quarter * (period // 4)
    angle = rest.astype(jnp.float32) * (2.0 * math.pi / period)
    square = angle * angle
    sin = -1.0 / 5040 + square * (1.0 / 362880)
    sin = -1.0 / 6 + square * (1.0 / 120 + square * sin)
    sin = angle + angle * square * sin
    cos = -1.0 / 720 + square * (1.0 / 40320)
    cos = 1.0 + square * (-0.5 + square * (1.0 / 24 + square * cos))
    odd = (quarter & 1) == 1
    full_cos, full_sin = jnp.where(odd, sin, cos), jnp.where(odd, cos, sin)
    full_cos = jnp.where(((quarter + 1) & 2) == 2, -full_cos, full_cos)
    return full_cos, jnp.where((quarter & 2) == 2, -full_sin, full_sin)


def tables_kernel(facet_ref, listed_ref, count_ref, *refs, period):
    table_ref, turn_ref, keep_ref = refs[-3:]
    facet = facet_ref[0]
    span = period // SG
    cells = PACK * SG
    row = lax.broadcasted_iota(jnp.int32, (cells, LANES), 0)
    lane = lax.broadcasted_iota(jnp.int32, (cells, LANES), 1)
    tiles = table_ref.shape[1] // LANES
    room = LANES // PACK
    turn_shape = (FY, 2 * PACK * SG)
    turn_line = lax.broadcasted_iota(jnp.int32, turn_shape, 0) - FY // 2
    turn_lane = lax.broadcasted_iota(jnp.int32, turn_shape, 1)
    second = (turn_lane >> 5 & 1) == 1

    def col_cell(group):
        sub = group * PACK + (row >> 5)
        return (wrapped(sub * 53 + 5, span) - span // 2) * SG + (row & (SG - 1))

    tile_id = lane & (room - 1)
    start = jnp.where(tile_id == tiles - 1, -MARGIN, tile_id * LANES)
    start = facet * FX - period // 2 + start
    for batch in range(SETS // PACK):
        coarse_cos, coarse_sin = circle(col_cell(batch * PACK + (lane >> 5)) * start, period)
        for k in range(PACK):
            group = batch * PACK + k
            base = group * 2 * cells
            fine_cos, fine_sin = circle(col_cell(group) * lane, period)
            for tile in range(tiles):
                columns = slice(tile * LANES, (tile + 1) * LANES)
                at = k * room + tile
                tile_cos = coarse_cos[:, at : at + 1]
                tile_neg = -coarse_sin[:, at : at + 1]
                full_cos = tile_cos * fine_cos + tile_neg * fine_sin
                full_neg = tile_neg * fine_cos - tile_cos * fine_sin
                table_ref[base : base + cells, columns] = full_cos.astype(jnp.bfloat16)
                table_ref[base + cells : base + 2 * cells, columns] = full_neg.astype(
                    jnp.bfloat16
                )

            sub = group * PACK + (turn_lane >> 6)
            cell = (wrapped(sub * 37, span) - span // 2) * SG + (turn_lane & (SG - 1))
            cos, sin = circle(cell * turn_line, period)
            turn_ref[group, :FY] = jnp.where(second, -sin, cos).astype(jnp.bfloat16)
            turn_ref[group, FY:] = jnp.where(second, cos, sin).astype(jnp.bfloat16)

    line = lax.broadcasted_iota(jnp.int32, (FY, MARGIN), 0)
    before = jnp.maximum(facet - 1, 0)
    in_use = jnp.where(facet > 0, count_ref[before], 0)

    def mark(k, keep):
        return jnp.where((line == listed_ref[before, k]) & (k < in_use), 1.0, keep)

    keep_ref[...] = lax.fori_loop(
        0, listed_ref.shape[1], mark, jnp.zeros((FY, MARGIN), jnp.float32)
    )


def make_tables(facet, listed, counts, period, token):
    depth, width = 2 * NSUB * SG, FX + MARGIN
    vmem = pl.BlockSpec(memory_space=pltpu.VMEM)
    return pl.pallas_call(
        functools.partial(tables_kernel, period=period),
        out_shape=[
            jax.ShapeDtypeStruct((depth, width), jnp.bfloat16),
            jax.ShapeDtypeStruct((SETS, 2 * FY, 2 * PACK * SG), jnp.bfloat16),
            jax.ShapeDtypeStruct((FY, MARGIN), jnp.float32),
        ],
        grid_spec=pltpu.PrefetchScalarGridSpec(
            num_scalar_prefetch=3,
            grid=(),
            in_specs=[pl.BlockSpec(memory_space=pl.ANY)],
            out_specs=[vmem] * 3,
        ),
        compiler_params=pltpu.CompilerParams(vmem_limit_bytes=16 << 20),
        cost_estimate=pl.CostEstimate(
            flops=8 * depth * width, bytes_accessed=2 * depth * width, transcendentals=1 << 19
        ),
        name="make_tables",
    )(facet, listed, counts, token)


def image_kernel(z1_ref, z0_ref, x_ref, *refs, places, scale, columns):
    parts = len(places)
    piece_refs = refs[:parts]
    turn_ref, table_ref, keep_ref = refs[parts : parts + 3]
    out_ref, lines_ref, done_ref, sems = refs[-4:]
    per = piece_refs[0].shape[0]
    width = table_ref.shape[1] - MARGIN
    slot = lax.broadcasted_iota(jnp.int32, (2 * SG, 2 * LANES), 1) % LANES // SG
    flat = [(part, i) for part in range(parts) for i in range(per)]

    def group_rows(group):
        base = group * 2 * LANES
        for k in range(0, len(flat), 2):
            pair = [piece_refs[part][i, group] for part, i in flat[k : k + 2]]
            pair = jnp.concatenate(pair, axis=1)
            zero = jnp.zeros_like(pair)
            spread = [jnp.where(slot[:, : pair.shape[1]] == s, pair, zero) for s in range(PACK)]
            spread = jnp.concatenate(spread, axis=0)
            turned = jnp.dot(turn_ref[group], spread, preferred_element_type=jnp.float32)
            turned = (turned * scale).astype(jnp.bfloat16)
            for m in range(pair.shape[1] // LANES):
                for q in range(2):
                    lines_ref[
                        (k + m) * FY : (k + m + 1) * FY, base + q * LANES : base + (q + 1) * LANES
                    ] = turned[q * FY : (q + 1) * FY, m * LANES : (m + 1) * LANES]

    for group in range(SETS):
        group_rows(group)
    lines = lines_ref[...]

    def spot(part):
        z_step, x_step, east, half = places[part]
        share = lax.rem(z0_ref[0] + z1_ref[0] + z_step, 2) * east
        share = share + lax.rem(x_ref[0] + east - x_step, east)
        return (share * 2 + half) * per

    def copy(step, part):
        return pltpu.make_async_copy(
            done_ref.at[step % 2, pl.ds(part * per, per)],
            out_ref.at[pl.ds(spot(part), per), :, pl.ds(step * columns, columns)],
            sems.at[step % 2, part],
        )

    steps = width // columns
    for step in range(steps):
        if step >= 2:
            for part in range(parts):
                copy(step - 2, part).wait()
        block = table_ref[:, step * columns : (step + 1) * columns]
        total = jnp.dot(lines, block, preferred_element_type=jnp.float32)
        done_ref[step % 2] = total.reshape(parts * per, FY, columns)
        if step == 0:
            edge = jnp.dot(lines, table_ref[:, width:], preferred_element_type=jnp.float32)
            edge = edge.reshape(parts * per, FY, MARGIN) * keep_ref[...][None]
            done_ref[0, :, :, :MARGIN] += edge
        for part in range(parts):
            copy(step, part).start()
    for step in range(max(steps - 2, 0), steps):
        for part in range(parts):
            copy(step, part).wait()


def add_image(image, device, places, pieces, turn, table, keep, total_pols, scale, after):
    parts, per = len(pieces), pieces[0].shape[0]
    pols = parts * per
    columns = 1024
    depth = table.shape[0]
    width = table.shape[1] - MARGIN
    vmem = pl.BlockSpec(memory_space=pltpu.VMEM)
    operands = [*pieces, turn, table, keep]
    in_specs = [vmem] * len(operands)
    operands.extend(after)
    in_specs.extend([pl.BlockSpec(memory_space=pl.ANY)] * len(after))
    aliases = {}
    if image is not None:
        operands.append(image)
        in_specs.append(pl.BlockSpec(memory_space=pl.ANY))
        aliases = {len(operands) + 2: 0}
    return pl.pallas_call(
        functools.partial(image_kernel, places=places, scale=scale, columns=columns),
        out_shape=jax.ShapeDtypeStruct((total_pols, FY, width), jnp.float32),
        grid_spec=pltpu.PrefetchScalarGridSpec(
            num_scalar_prefetch=3,
            grid=(),
            in_specs=in_specs,
            out_specs=pl.BlockSpec(memory_space=pl.ANY),
            scratch_shapes=[
                pltpu.VMEM((pols * FY, depth), jnp.bfloat16),
                pltpu.VMEM((2, pols, FY, columns), jnp.float32),
                pltpu.SemaphoreType.DMA((2, parts)),
            ],
        ),
        input_output_aliases=aliases,
        compiler_params=pltpu.CompilerParams(vmem_limit_bytes=28 << 20),
        cost_estimate=pl.CostEstimate(
            flops=2 * pols * FY * depth * width,
            bytes_accessed=2 * depth * width + 4 * pols * FY * width,
            transcendentals=0,
        ),
        name="add_image",
    )(*device, *operands)


def shards(
    visibilities, w_kernel, w_index, cell_offsets, block_sub, intersection_rows, intersection_count
):
    cores, east = lax.axis_size("core"), lax.axis_size("x")
    north, upper = lax.axis_size("y"), lax.axis_size("z0")
    groups, facets = north * cores, lax.axis_size(FACET)
    num_chans, num_parts, _, row_len = visibilities.shape
    num_pols = num_parts // 2
    own_chans = num_chans // groups
    shares = upper * east
    chan_shares = math.gcd(shares, own_chans)
    pol_shares = shares // chan_shares
    per_chan, per_pol = own_chans // chan_shares, num_pols // pol_shares
    lines = 2 * per_chan * per_pol
    period = FX * facets
    z1, z0, x = (lax.axis_index(axis) for axis in ("z1", "z0", "x"))

    def scalar(value):
        return jnp.reshape(value, (1,)).astype(jnp.int32)

    vis = visibilities.reshape(num_chans, num_parts, row_len)
    inner = ("y", "z0", "x")
    apart = north == upper == east == 2
    sent = pack_rows(
        [scalar(lax.axis_index(CHAN)), scalar(lax.axis_index(inner)), scalar(z1)],
        vis,
        w_index,
        cell_offsets,
        block_sub,
        (chan_shares, pol_shares, per_chan, per_pol, cores, east),
        north * shares,
        lines,
        apart,
    )
    if apart:
        rows = [sent[0]]
        for k in range(1, len(sent)):
            route = [(i, i ^ k) for i in range(len(sent))]
            rows.append(lax.ppermute(sent[k], inner, route))
    else:
        rows = [lax.all_to_all(sent[0], inner, split_axis=0, concat_axis=0, tiled=True)]
    taps = w_kernel.transpose(1, 2, 0).reshape(-1, w_kernel.shape[0])
    place = scalar(lax.axis_index("core"))
    scale = 1.0 / math.sqrt(groups * facets * row_len)

    def gridded(half, after):
        parts = len(rows)
        ids = [rows[k % (parts // 2)] for k in range(parts)] if parts > 1 else rows
        slots = [k * 2 // parts for k in range(parts)]
        begun, begin = None, 0
        if half == 0 and parts > 1:
            begun, begin = grid_rows(
                place,
                taps,
                rows[: parts // 2],
                ids[: parts // 2],
                slots[: parts // 2],
                row_len,
                half,
                after,
                ends=False,
            )[0], parts // 2
        own, other = grid_rows(
            place, taps, rows[begin:], ids[begin:], slots[begin:], row_len, half, after, begun
        )
        return own, swap(other, "core")

    def shifted(piece, z_step, x_step):
        if z_step + x_step == 0:
            return piece
        route = [
            (a * east + b, (a + z_step) % upper * east + (b + x_step) % east)
            for a in range(upper)
            for b in range(east)
        ]
        return lax.ppermute(piece, ("z0", "x"), route)

    def gathered(mine, relay):
        pieces = []
        for z_step in range(upper):
            here = shifted(mine, z_step, 0)
            for x_step in range(east):
                if relay or z_step + x_step == 0:
                    pieces.append(shifted(here, 0, x_step))
                else:
                    pieces.append(shifted(mine, z_step, x_step))
        return pieces

    def mirrored(block):
        return lax.ppermute(block, ("z1", "z0"), [(i, 3 - i) for i in range(4)])

    first = add(gridded(0, ()))
    first_far = mirrored(first)
    second = gridded(1, (first,))
    first = add((first, first_far), second[:1])
    second = add(second, (first,))
    second_far = mirrored(second)
    first_pieces = gathered(first, False)
    table, turn, keep = make_tables(
        scalar(lax.axis_index(FACET)), intersection_rows, intersection_count, period, first
    )
    second = add((second, second_far))
    second_pieces = gathered(second, False)
    total_pols = own_chans * num_pols
    device = [scalar(lax.axis_index(axis)) for axis in ("z1", "z0", "x")]
    places = [
        [(a, b, east, half) for a in range(upper) for b in range(east)] for half in range(2)
    ]
    pieces = first_pieces + second_pieces
    places = places[0] + places[1]
    parts = len(first_pieces)
    image = None
    calls = (
        [*range(parts - 1), parts],
        [parts - 1, *range(parts + 1, 2 * parts - 1)],
        [2 * parts - 1],
    )
    for chosen in calls:
        image = add_image(
            image,
            device,
            [places[k] for k in chosen],
            [pieces[k] for k in chosen],
            turn,
            table,
            keep,
            total_pols,
            scale,
            (second,),
        )
    return image.reshape(own_chans, num_pols, FY, FX)


def solution(mesh):
    groups, facets = mesh.shape["chan"], mesh.shape["facet"]
    inner = Mesh(
        mesh.devices.reshape(groups // 2, 2, 2, 2, facets // 4), CHAN + FACET
    )
    return jax.shard_map(
        shards,
        mesh=inner,
        in_specs=(
            P(None, None, CHAN, FACET),
            P(),
            P(None, FACET),
            P(None, None, FACET),
            P(None, FACET),
            P(),
            P(),
        ),
        out_specs=P(CHAN, None, None, FACET),
        check_vma=False,
    )
```
